256 devices in a mesh: leaf: 32 (over z, y), grid: 8 (over x, core).
Axes of the slice: x: 4, y: 4, z: 8, core: 2. Of those that a mesh axis runs over, the one named last changes fastest.
Arguments:
- top_solution: bfloat16 [4096, 256], P(('leaf', 'grid')), may hold values from -6 to 6
- right_one: bfloat16 [32, 1024, 256], P('leaf', 'grid'), may hold values from -6 to 6
- update_one: bfloat16 [32, 2048, 1024], P('leaf', None, 'grid'), may hold values from -0.125 to 0.125
- inverse_one: bfloat16 [32, 1024, 1024], P('leaf', None, 'grid'), as said below
- top_rows_one: int32 [32, 2048], P('leaf'), may hold values from 0 to 4095, as said below
- live_one: int32 [32], P('leaf'), may hold values from 512 to 1024
- right_two: bfloat16 [384, 1024, 256], P('leaf', 'grid'), may hold values from -6 to 6
- update_two: bfloat16 [384, 2048, 1024], P('leaf', None, 'grid'), may hold values from -0.125 to 0.125
- inverse_two: bfloat16 [384, 1024, 1024], P('leaf', None, 'grid'), as said below
- top_rows_two: int32 [384, 1536], P('leaf'), may hold values from 0 to 4095, as said below
- sep_rows: int32 [384, 512], P('leaf'), may hold values from 0 to 1023, as said below
- parent: int32 [384], P('leaf'), may hold values from 0 to 31, as said below
- live_two: int32 [384], P('leaf'), may hold values from 512 to 1024
Outputs:
- solution_one: bfloat16 [32, 1024, 256], P('leaf', 'grid')
- solution_two: bfloat16 [384, 1024, 256], P('leaf', 'grid')
The draws below stay inside these ranges and needn't reach their ends.
Inputs may be any that keep to these rules, and one draw needn't show every extreme that they name: `top_rows_one`: each row lists 2048 distinct rows in increasing order. `top_rows_two`: each row lists 1536 distinct rows in increasing order. `sep_rows`: each row lists 512 distinct rows of the parent's separator in increasing order. The parent of level-two front f differs from f // 12 by at most one; in each group of 12 fronts, one of the first two has parent f // 12 - 1 and the other f // 12 + 1, where these exist. `inverse_one`: zero above the diagonal. `inverse_two`: zero above the diagonal.
All inputs are finite; a program needn't handle non-finite values.
Results may differ from the reference program's by a relative error of at most 0.0053.
Values may be sent and summed in bfloat16 or wider, within the bound.
A program may use at most 128 MiB of HBM per device.

```python
import math
import jax
import jax.numpy as jnp
from jax import lax

R = 256
S = 1024
UT = 1536
UP = 512
NT = 4096
C2 = 12
U = 2048
F1 = 32
F2 = 384


def distinct_rows(key, fronts, count, pool):
    scores = jax.random.randint(key, (fronts, pool), 0, 1 << 18) * pool + jnp.arange(pool, dtype=jnp.int32)[None, :]
    chosen = lax.top_k(scores, count)[1]
    return jnp.sort(chosen, axis=1).astype(jnp.int32)


def triangular_inverse(key, fronts):

    def one_front(front_index):
        front_key = jax.random.fold_in(key, front_index)
        key_normal = jax.random.fold_in(front_key, 0)
        key_diagonal = jax.random.fold_in(front_key, 2)
        normal_part = jax.random.normal(key_normal, (S, S), jnp.float32)
        off_diagonal = normal_part
        diagonal = jax.random.uniform(key_diagonal, (S,), jnp.float32, 0.5, 1.5)
        row_index = lax.broadcasted_iota(jnp.int32, (S, S), 0)
        col_index = lax.broadcasted_iota(jnp.int32, (S, S), 1)
        lower_part = jnp.where(row_index > col_index, off_diagonal * (0.8 / math.sqrt(S)), 0.0)
        main_part = jnp.where(row_index == col_index, diagonal[:, None], 0.0)
        return (lower_part + main_part).astype(jnp.bfloat16)
    return lax.map(one_front, jnp.arange(fronts, dtype=jnp.int32))


def draw_inverse_one(key, part):
    key = jax.random.fold_in(key, 3)
    return triangular_inverse(key, F1)


def draw_inverse_two(key, part):
    key = jax.random.fold_in(key, 5)
    return triangular_inverse(key, F2)


def draw_top_rows_one(key, part):
    key = jax.random.fold_in(key, 11)
    return distinct_rows(key, F1, U, NT)


def draw_top_rows_two(key, part):
    key = jax.random.fold_in(key, 12)
    return distinct_rows(key, F2, UT, NT)


def draw_sep_rows(key, part):
    key = jax.random.fold_in(key, 13)
    return distinct_rows(key, F2, UP, S)


def draw_parent(key, part):
    key = jax.random.fold_in(key, 14)
    key_offsets, key_flips = jax.random.split(key, 2)
    offsets = jax.random.randint(key_offsets, (F2,), -1, 2)
    flips = jax.random.randint(key_flips, (F1,), 0, 2)
    owners = jnp.arange(F2, dtype=jnp.int32) // C2
    slot_index = jnp.arange(F2, dtype=jnp.int32) % C2
    first_side = jnp.where(jnp.take(flips, owners) == 1, -1, 1)
    offsets = jnp.where(slot_index == 0, first_side, jnp.where(slot_index == 1, -first_side, offsets))
    return jnp.clip(owners + offsets, 0, F1 - 1).astype(jnp.int32)


def touch_ends(drawn, key, least, top_value):
    dims = drawn.shape
    spot = [jax.random.randint(jax.random.fold_in(key, axis), (), 0, dims[axis]) for axis in range(len(dims))]
    drawn = drawn.at[tuple(spot)].set(least)
    longest = dims.index(max(dims))
    spot[longest] = (spot[longest] + 1) % dims[longest]
    return drawn.at[tuple(spot)].set(top_value)


def steps_of(stream_key, dims, cuts, least, top_value):
    def one(dim, shards_of):
        draws = jax.random.uniform(jax.random.fold_in(jax.random.fold_in(stream_key, 6), dim), (shards_of,), jnp.float32, least / len(cuts), top_value / len(cuts))
        return jnp.repeat(jnp.exp(draws), dims[dim] // shards_of).reshape((-1,) + (1,) * (len(dims) - dim - 1))

    gain = one(*cuts[0])
    for cut in cuts[1:]:
        gain = gain * one(*cut)
    return gain


def scatter_about(key, extent, spread, reach, cuts=(), kind=jnp.bfloat16):
    gain = steps_of(key, extent, cuts, -0.22, 0.18) if cuts else 1.0
    drawn = jax.random.normal(key, extent, jnp.float32) * spread * gain
    return jnp.minimum(jnp.maximum(drawn, -reach), reach).astype(kind)


def setup_inputs(seed: int = 0) -> dict:
    key_of = jax.random.split(jax.random.key(seed), 14)
    return {
        "top_solution": scatter_about(key_of[0], (NT, R), 1.0, 6.0, ((0, 256),)),
        "right_one": scatter_about(key_of[1], (F1, S, R), 1.0, 6.0, ((0, 32), (1, 8))),
        "update_one": scatter_about(key_of[2], (F1, U, S), U ** -0.5, 0.125, ((0, 32), (2, 8))),
        "inverse_one": draw_inverse_one(jax.random.fold_in(key_of[13], 71), 0),
        "top_rows_one": draw_top_rows_one(jax.random.fold_in(key_of[13], 71), 0),
        "live_one": touch_ends(jax.random.randint(key_of[5], (F1,), S // 2, S + 1), jax.random.fold_in(key_of[5], 1), S // 2, S).astype(jnp.int32),
        "right_two": scatter_about(key_of[6], (F2, S, R), 1.0, 6.0, ((0, 32), (1, 8))),
        "update_two": scatter_about(key_of[7], (F2, U, S), U ** -0.5, 0.125, ((0, 32), (2, 8))),
        "inverse_two": draw_inverse_two(jax.random.fold_in(key_of[13], 71), 0),
        "top_rows_two": draw_top_rows_two(jax.random.fold_in(key_of[13], 71), 0),
        "sep_rows": draw_sep_rows(jax.random.fold_in(key_of[13], 71), 0),
        "parent": draw_parent(jax.random.fold_in(key_of[13], 71), 0),
        "live_two": touch_ends(jax.random.randint(key_of[12], (F2,), S // 2, S + 1), jax.random.fold_in(key_of[12], 1), S // 2, S).astype(jnp.int32),
    }


def solve_front(factor, inverse, right_side, gathered, live_rows):
    product = jnp.dot(factor.astype(jnp.float32).T, gathered.astype(jnp.float32), preferred_element_type=jnp.float32)
    reduced = (right_side.astype(jnp.float32) - product).astype(jnp.bfloat16)
    solved = jnp.dot(inverse.astype(jnp.float32).T, reduced.astype(jnp.float32), preferred_element_type=jnp.float32)
    positions = jnp.arange(solved.shape[0], dtype=jnp.int32)
    return jnp.where((positions < live_rows)[:, None], solved, 0.0).astype(jnp.bfloat16)


def reference(top_solution, right_one, update_one, inverse_one, top_rows_one, live_one, right_two, update_two, inverse_two, top_rows_two, sep_rows, parent, live_two):
    def level_one_front(front_items):
        top_picks, factor, inverse, right_side, live_rows = front_items
        gathered = jnp.take(top_solution, top_picks, axis=0)
        return solve_front(factor, inverse, right_side, gathered, live_rows)

    level_one = lax.map(level_one_front, (top_rows_one, update_one, inverse_one, right_one, live_one))

    def level_two_front(front_items):
        top_picks, sep_picks, parent_index, factor, inverse, right_side, live_rows = front_items
        from_top = jnp.take(top_solution, top_picks, axis=0)
        parent_block = lax.dynamic_index_in_dim(level_one, parent_index.astype(jnp.int32), 0, keepdims=False)
        from_parent = jnp.take(parent_block, sep_picks, axis=0)
        gathered = jnp.concatenate([from_top, from_parent], axis=0)
        return solve_front(factor, inverse, right_side, gathered, live_rows)

    second = lax.map(level_two_front, (top_rows_two, sep_rows, parent, update_two, inverse_two, right_two, live_two))
    return (level_one, second)
```

```python
import functools

import jax
import jax.numpy as jnp
from jax import lax
from jax.experimental import pallas as pl
from jax.experimental.pallas import tpu as pltpu
from jax.sharding import PartitionSpec as P

MESH = pl.DeviceIdType.MESH
F32 = jnp.float32
BF = jnp.bfloat16

R = 256
B = 128
S = 1024
U = 2048
UT = 1536
UP = 512
C2 = 12
NX, NY, NZ = 4, 4, 8
LEAVES = NY * NZ
BS = 512
BD = 256

ONE = C2
LAG_B, LAG_C, LAG_D, LAG_E = 6, 8, 10, 12


def kernel(
    top, right1, upd1, inv1, rows1, right2, upd2, inv2, rows2, seps, parent_s, live1_s, live2_s,
    out1, out2,
    topb, topT, u1, i1, r1, t1, t1s, u2, i2, r2, t2, t2s, sp,
    acc, rbuf, s1, ob1, ob2,
    ld, ldsem_out,
    g_send, g_recv, a_send, a_recv, c_send, c_recv,
    x_send, x_recv, k_send, k_recv,
    nb_send, nb_recv, sx_send, sx_recv, sk_send, sk_recv,
):
    leaf = lax.axis_index("leaf")
    g = lax.axis_index("grid")
    z, y = leaf // NY, leaf % NY
    x, c = g // 2, g % 2
    sib = (leaf, x * 2 + (1 - c))

    def at_x(xx):
        return (leaf, xx * 2 + c)

    def rcopy(src, dst, ssem, rsem, dev):
        return pltpu.make_async_remote_copy(
            src_ref=src, dst_ref=dst, send_sem=ssem, recv_sem=rsem, device_id=dev, device_id_type=MESH
        )

    def same(ref, ssem, rsem, dev):
        return rcopy(ref, ref, ssem, rsem, dev)

    own_rows = topb.at[pl.ds(pl.multiple_of(g * 16, 16), 16), :]
    loads = [
        (top, own_rows),
        (upd1.at[0], u1),
        (rows1, t1s),
        (right1.at[0], r1),
        (inv1.at[0], i1),
        (rows2, t2s),
        (upd2, u2),
        (seps, sp),
        (right2, r2),
        (inv2, i2),
    ]
    loads += [(rows1.at[:, pl.ds(d * BD, BD)], t1.at[d]) for d in range(U // BD)]
    loads += [(rows2.at[:, pl.ds(d * BD, BD)], t2.at[d]) for d in range(UT // BD)]
    loads = [pltpu.make_async_copy(a, b, ld.at[i]) for i, (a, b) in enumerate(loads)]
    for copy in loads:
        copy.start()

    barrier = pltpu.get_barrier_semaphore()

    def greet(dev):
        pl.semaphore_signal(barrier, inc=1, device_id=dev, device_id_type=MESH)

    for d in range(1, 8):
        greet((leaf, (g + d) % 8))
    for d in range(1, NY):
        greet((z * NY + (y + d) % NY, g))
    for d in range(1, NZ):
        greet((((z + d) % NZ) * NY + y, g))

    @pl.when(leaf > 0)
    def _():
        greet((leaf - 1, g))

    @pl.when(leaf < LEAVES - 1)
    def _():
        greet((leaf + 1, g))

    for k in range(7):

        @pl.when(jnp.logical_and(k < g, jnp.logical_not(jnp.logical_and(g == 7, k == 5))))
        def _():
            def zero(f, carry):
                rbuf[f, k] = jnp.zeros((R, B), BF)
                return carry

            lax.fori_loop(0, C2 + 1, zero, 0)

    ends = jnp.where(leaf > 0, 1, 0) + jnp.where(leaf < LEAVES - 1, 1, 0)
    pl.semaphore_wait(barrier, 7 + (NY - 1) + (NZ - 1) + ends)

    loads[0].wait()
    for d in range(1, 8):
        rcopy(own_rows, own_rows, g_send.at[d - 1], g_recv.at[d - 1], (leaf, (g + d) % 8)).start()
    for d in range(1, 8):
        other = (g + 8 - d) % 8
        part = topb.at[pl.ds(pl.multiple_of(other * 16, 16), 16), :]
        same(part, g_send.at[d - 1], g_recv.at[d - 1], (leaf, other)).wait_recv()
    block = topb[...].astype(F32).T.astype(BF)
    topT[z, y] = block.reshape(2, 128, B)

    def yz(zz, yy):
        return (((zz + NZ) % NZ) * NY + (yy + NY) % NY, g)

    def hand(region, i):
        same(region, c_send.at[i], c_recv.at[i], sib).start()

    def pieces0():
        out = [topT.at[z, (y + NY - d) % NY, 0] for d in (1, 3, 2)]
        out += [topT.at[(z + NZ - k) % NZ, :, 0] for k in (1, 2, 3)] + [topT.at[(z + 4) % NZ, pl.ds(0, 2), 0]]
        out += [topT.at[(z + k) % NZ, :, 0] for k in (1, 2, 3)] + [topT.at[(z + 4) % NZ, pl.ds(2, 2), 0]]
        return out

    def pieces1():
        out = [topT.at[(z + NZ - i) % NZ, y, 1] for i in range(1, NZ)]
        out += [topT.at[:, (y + NY - 1) % NY, 1], topT.at[:, (y + 1) % NY, 1]]
        out += [topT.at[pl.ds(0, 4), (y + 2) % NY, 1], topT.at[pl.ds(4, 4), (y + 2) % NY, 1]]
        return out

    @pl.when(c == 0)
    def _():
        got = pieces0()

        def send(region, i, dev):
            same(region, a_send.at[i], a_recv.at[i], dev).start()

        def arrived(i):
            same(got[i], a_send.at[i], a_recv.at[i], sib).wait_recv()

        for i, d in enumerate((1, 3, 2)):
            send(topT.at[z, y, 0], i, yz(z, y + d))
        for i in range(3):
            arrived(i)
        for k in range(1, 5):
            right_src, left_src = topT.at[(z + NZ - k + 1) % NZ], topT.at[(z + k - 1) % NZ]
            if k < 4:
                send(right_src.at[:, 0], 2 + k, yz(z + 1, y))
                send(left_src.at[:, 0], 6 + k, yz(z - 1, y))
            else:
                send(right_src.at[pl.ds(0, 2), 0], 2 + k, yz(z + 1, y))
                send(left_src.at[pl.ds(2, 2), 0], 6 + k, yz(z - 1, y))
            if k == 1:
                for i in range(3):
                    hand(got[i], i)
            else:
                hand(got[1 + k], 1 + k)
                hand(got[5 + k], 5 + k)
            arrived(2 + k)
            arrived(6 + k)
        hand(got[6], 6)
        hand(got[10], 10)
        for i, region in enumerate(got):
            same(region, a_send.at[i], a_recv.at[i], sib).wait_send()
            same(region, c_send.at[i], c_recv.at[i], sib).wait_send()
        for i, region in enumerate(pieces1()):
            same(region, c_send.at[i], c_recv.at[i], sib).wait_recv()

    @pl.when(c == 1)
    def _():
        got = pieces1()

        def send(region, i, dev):
            same(region, a_send.at[i], a_recv.at[i], dev).start()

        def arrived(i):
            same(got[i], a_send.at[i], a_recv.at[i], sib).wait_recv()

        for i in (4, 3, 5, 2, 6, 1, 7):
            send(topT.at[z, y, 1], i - 1, yz(z + i, y))
        for i in range(7):
            arrived(i)
        send(topT.at[:, y, 1], 7, yz(z, y + 1))
        send(topT.at[:, y, 1], 8, yz(z, y - 1))
        for i in range(7):
            hand(got[i], i)
        arrived(7)
        send(topT.at[pl.ds(0, 4), (y + NY - 1) % NY, 1], 9, yz(z, y + 1))
        arrived(8)
        send(topT.at[pl.ds(4, 4), (y + 1) % NY, 1], 10, yz(z, y - 1))
        hand(got[7], 7)
        hand(got[8], 8)
        arrived(9)
        hand(got[9], 9)
        arrived(10)
        hand(got[10], 10)
        for i, region in enumerate(got):
            same(region, a_send.at[i], a_recv.at[i], sib).wait_send()
            same(region, c_send.at[i], c_recv.at[i], sib).wait_send()
        for i, region in enumerate(pieces0()):
            same(region, c_send.at[i], c_recv.at[i], sib).wait_recv()

    for copy in loads[1:]:
        copy.wait()

    def picked_product(count, front, vec, sca, factor):
        nd, ns = count // BD, (LEAVES * B) // BS
        total = jnp.zeros((R, B), F32)
        firsts = [sca[front, i * BD] for i in range(1, nd)]
        passed_at = []
        for i, v in enumerate(firsts):
            ends = jnp.int32(i)
            for j in range(1, ns):
                ends = ends + jnp.where(v >= j * BS, 1, 0)
            passed_at.append(ends)
        iota = lax.broadcasted_iota(jnp.int32, (BS, BD), 0)
        for t in range(nd + ns - 1):
            d = jnp.int32(0)
            for ends in passed_at:
                d = d + jnp.where(ends < t, 1, 0)
            s = t - d
            src = topT[s]
            lhs = jnp.concatenate([src[i].reshape(R, B) for i in range(BS // B)], axis=1)
            picks = vec[d, pl.ds(front, 1), :]
            onehot = jnp.where(iota == picks - s * BS, 1.0, 0.0).astype(BF)
            got = jnp.dot(lhs, onehot, preferred_element_type=F32).astype(BF)
            total = total + jnp.dot(got, factor(d), preferred_element_type=F32)
        return total

    def xs(f, i, k, dest):
        return same(rbuf.at[f, 2 * k + c], x_send.at[f, i], x_recv.at[f, k], at_x(dest))

    def ks(f, k, core):
        return same(rbuf.at[f, 2 * k + core], k_send.at[f, k], k_recv.at[f, k], sib)

    def x_arrived(f, k):
        xs(f, 0, k, 0).wait_recv()

    def own_sends(f, act):
        @pl.when(x == 3)
        def _():
            act(xs(f, 0, 3, 2))
            act(xs(f, 1, 3, 0))

        @pl.when(x == 2)
        def _():
            act(xs(f, 0, 2, 1))

            @pl.when(c == 1)
            def _():
                act(xs(f, 1, 2, 3))

        @pl.when(x == 1)
        def _():
            act(xs(f, 0, 1, 0))

        @pl.when(c == 1)
        def _():
            act(ks(f, x, c))

    def first_hop(f, wait, act):
        @pl.when(x == 0)
        def _():
            wait(f, 3)
            act(xs(f, 0, 3, 1))
            act(ks(f, 3, c))
            wait(f, 1)
            act(ks(f, 1, c))

        @pl.when(x == 1)
        def _():
            wait(f, 2)

            @pl.when(c == 0)
            def _():
                act(xs(f, 1, 2, 0))

            act(ks(f, 2, c))

        @pl.when(x == 2)
        def _():
            wait(f, 3)
            act(ks(f, 3, c))

        @pl.when(jnp.logical_and(x == 3, c == 1))
        def _():
            wait(f, 2)
            act(xs(f, 2, 2, 0))

    def second_hop(f, wait, act):
        @pl.when(x == 0)
        def _():
            wait(f, 2)
            act(ks(f, 2, c))

        @pl.when(x == 1)
        def _():
            wait(f, 3)
            act(ks(f, 3, c))

    def from_core(f):
        for k in range(4):

            @pl.when(jnp.logical_or(k > x, jnp.logical_and(k == x, c == 0)))
            def _():
                ks(f, k, 1 - c).wait_recv()

    def start(copy):
        copy.start()

    def drain(copy):
        copy.wait_send()

    def nothing(f, k):
        pass

    lanes = lax.broadcasted_iota(jnp.int32, (R, B), 1) + g * B

    def solve(f, inverse, live):
        lhs = jnp.concatenate([rbuf[f, k] for k in range(8)], axis=1)
        solved = jnp.dot(lhs, inverse, preferred_element_type=F32)
        return jnp.where(lanes < live, solved, 0.0)

    total1 = picked_product(U, 0, t1, t1s, lambda d: u1[d])
    rbuf[ONE, g] = (r1[...].astype(F32).T - total1).astype(BF)
    own_sends(ONE, start)

    def s1_x(slot, d):
        return same(s1.at[slot, g], sx_send.at[slot, d - 1], sx_recv.at[slot, d - 1], at_x((x + d) % NX))

    def s1_x_got(slot, d):
        return s1.at[slot, 2 * ((x + NX - d) % NX) + c]

    def s1_k(slot, k, core):
        return same(s1.at[slot, 2 * k + core], sk_send.at[slot, k], sk_recv.at[slot, k], sib)

    def with_slots(slots, body):
        for slot in slots:
            if slot == 1:
                body(slot)
            else:

                @pl.when((leaf > 0) if slot == 0 else (leaf < LEAVES - 1))
                def _():
                    body(slot)

    def s1_up():
        return rcopy(s1.at[1, g], s1.at[0, g], nb_send.at[0], nb_recv.at[0], (leaf + 1, g))

    def s1_down():
        return rcopy(s1.at[1, g], s1.at[2, g], nb_send.at[1], nb_recv.at[1], (leaf - 1, g))

    def solve_one():
        from_core(ONE)
        solved = solve(ONE, i1[...], live1_s[0])
        s1[1, g] = solved.astype(BF)

        @pl.when(leaf < LEAVES - 1)
        def _():
            s1_up().start()

        @pl.when(leaf > 0)
        def _():
            s1_down().start()

        spread(1)
        ob1[...] = solved.T.astype(BF)
        pltpu.make_async_copy(ob1, out1.at[0], ldsem_out.at[C2]).start()

    def spread(slot):
        for d in (2, 1, 3):
            s1_x(slot, d).start()
        s1_k(slot, x, c).start()

    def s1_neighbours():
        def body(slot):
            if slot == 0:
                s1_up().wait_recv()
            else:
                s1_down().wait_recv()
            spread(slot)

        with_slots((0, 2), body)

    def s1_cross(slots):
        def body(slot):
            for d in (1, 3, 2):
                same(s1_x_got(slot, d), sx_send.at[slot, d - 1], sx_recv.at[slot, d - 1], sib).wait_recv()
                s1_k(slot, (x + NX - d) % NX, c).start()

        with_slots(slots, body)

    def s1_end():
        def body(slot):
            for k in range(NX):
                s1_k(slot, k, 1 - c).wait_recv()

        with_slots((1, 0, 2), body)

    def top_part(f):
        acc[f] = picked_product(UT, f, t2, t2s, lambda d: u2[f, d])

    def parent_part(f):
        slot = jnp.clip(parent_s[f] - leaf + 1, 0, 2)
        block = s1[slot]
        lhs = jnp.concatenate([block[k] for k in range(8)], axis=1)
        total = acc[f]
        iota = lax.broadcasted_iota(jnp.int32, (S, BD), 0)
        for d in range(UP // BD):
            picks = sp[pl.ds(f, 1), pl.ds(d * BD, BD)]
            onehot = jnp.where(iota == picks, 1.0, 0.0).astype(BF)
            got = jnp.dot(lhs, onehot, preferred_element_type=F32).astype(BF)
            total = total + jnp.dot(got, u2[f, UT // BD + d], preferred_element_type=F32)
        rbuf[f, g] = (r2[f].astype(F32).T - total).astype(BF)
        own_sends(f, start)

    def solve_two(f):
        from_core(f)
        solved = solve(f, i2[f], live2_s[f])
        ob2[f] = solved.T.astype(BF)
        pltpu.make_async_copy(ob2.at[f], out2.at[f], ldsem_out.at[f]).start()

    def body(it, carry):
        pl.when(it == 1)(lambda: first_hop(ONE, x_arrived, start))
        pl.when(it == 2)(lambda: second_hop(ONE, x_arrived, start))
        pl.when(it == 3)(solve_one)

        @pl.when(it == 4)
        def _():
            s1_neighbours()
            s1_cross((1,))

        pl.when(it == 5)(lambda: s1_cross((0, 2)))
        pl.when(it == 6)(s1_end)

        def staged(lag, action):
            @pl.when(jnp.logical_and(it >= lag, it < C2 + lag))
            def _():
                action(it - lag)

        staged(LAG_C, lambda f: first_hop(f, x_arrived, start))
        staged(LAG_D, lambda f: second_hop(f, x_arrived, start))
        staged(LAG_B, parent_part)
        staged(LAG_E, solve_two)
        staged(0, top_part)
        return carry

    lax.fori_loop(0, C2 + LAG_E, body, 0)

    for d in range(1, 8):
        rcopy(own_rows, own_rows, g_send.at[d - 1], g_recv.at[d - 1], (leaf, (g + d) % 8)).wait_send()

    def finish(f, carry):
        own_sends(f, drain)
        first_hop(f, nothing, drain)
        second_hop(f, nothing, drain)
        return carry

    lax.fori_loop(0, C2 + 1, finish, 0)

    def finish_slot(slot):
        for d in range(1, 4):
            s1_x(slot, d).wait_send()
        for k in range(NX):
            s1_k(slot, k, c).wait_send()

    with_slots((0, 1, 2), finish_slot)

    @pl.when(leaf < LEAVES - 1)
    def _():
        s1_up().wait_send()

    @pl.when(leaf > 0)
    def _():
        s1_down().wait_send()

    pltpu.make_async_copy(ob1, out1.at[0], ldsem_out.at[C2]).wait()

    def finish_out(f, carry):
        pltpu.make_async_copy(ob2.at[f], out2.at[f], ldsem_out.at[f]).wait()
        return carry

    lax.fori_loop(0, C2, finish_out, 0)


def local(
    top_solution, right_one, update_one, inverse_one, top_rows_one, live_one,
    right_two, update_two, inverse_two, top_rows_two, sep_rows, parent, live_two,
):
    anywhere = pl.BlockSpec(memory_space=pl.ANY)
    scalar = pl.BlockSpec(memory_space=pltpu.SMEM)
    dma = pltpu.SemaphoreType.DMA
    vm = pltpu.VMEM
    return pl.pallas_call(
        kernel,
        out_shape=(
            jax.ShapeDtypeStruct((1, B, R), BF),
            jax.ShapeDtypeStruct((C2, B, R), BF),
        ),
        in_specs=[anywhere] * 10 + [scalar] * 3,
        out_specs=(anywhere, anywhere),
        scratch_shapes=[
            vm((B, R), BF),
            vm((NZ, NY, 2, 128, B), BF),
            vm((U // BD, BD, B), BF),
            vm((S, B), BF),
            vm((B, R), BF),
            vm((U // BD, 1, BD), jnp.int32),
            pltpu.SMEM((1, U), jnp.int32),
            vm((C2, U // BD, BD, B), BF),
            vm((C2, S, B), BF),
            vm((C2, B, R), BF),
            vm((UT // BD, C2, BD), jnp.int32),
            pltpu.SMEM((C2, UT), jnp.int32),
            vm((C2, UP), jnp.int32),
            vm((C2, R, B), F32),
            vm((C2 + 1, 8, R, B), BF),
            vm((3, 8, R, B), BF),
            vm((B, R), BF),
            vm((C2, B, R), BF),
            dma((24,)), dma((C2 + 1,)),
            dma((7,)), dma((7,)), dma((11,)), dma((11,)), dma((11,)), dma((11,)),
            dma((C2 + 1, 3)), dma((C2 + 1, 4)), dma((C2 + 1, 4)), dma((C2 + 1, 4)),
            dma((2,)), dma((2,)), dma((3, 3)), dma((3, 3)), dma((3, 4)), dma((3, 4)),
        ],
        compiler_params=pltpu.CompilerParams(
            collective_id=0, has_side_effects=True, vmem_limit_bytes=56 * 1024 * 1024
        ),
        cost_estimate=pl.CostEstimate(flops=20_000_000_000, bytes_accessed=12_000_000, transcendentals=0),
        name="adjoint_solve",
    )(
        top_solution, right_one, update_one.reshape(1, U // BD, BD, B), inverse_one, top_rows_one,
        right_two, update_two.reshape(C2, U // BD, BD, B), inverse_two, top_rows_two, sep_rows,
        parent, live_one, live_two,
    )


def solution(mesh):
    in_specs = (
        P(("leaf", "grid"), None),
        P("leaf", "grid", None),
        P("leaf", None, "grid"),
        P("leaf", None, "grid"),
        P("leaf", None),
        P("leaf"),
        P("leaf", "grid", None),
        P("leaf", None, "grid"),
        P("leaf", None, "grid"),
        P("leaf", None),
        P("leaf", None),
        P("leaf"),
        P("leaf"),
    )
    out_specs = (P("leaf", "grid", None), P("leaf", "grid", None))
    return jax.shard_map(local, mesh=mesh, in_specs=in_specs, out_specs=out_specs, check_vma=False)
```

```python
import functools

import jax
import jax.numpy as jnp
from jax import lax
from jax.experimental import pallas as pl
from jax.experimental.pallas import tpu as pltpu
from jax.sharding import PartitionSpec as P

MESH = pl.DeviceIdType.MESH
F32 = jnp.float32
BF = jnp.bfloat16

R = 256
B = 128
S = 1024
U = 2048
UT = 1536
UP = 512
C2 = 12
NX, NY, NZ = 4, 4, 8
LEAVES = NY * NZ
BS = 256
DELAY = 3
BD = 256

ONE = C2
H = S // 2
LAG_B, LAG_C, LAG_D, LAG_E = 6, 10, 11, 14


def kernel(
    top, right1, upd1, inv1, rows1, right2, upd2, inv2, rows2, seps, parent_s, live1_s, live2_s,
    out1, out2,
    topb, topT, u1, r1, t1, t1s, u2, r2, t2, t2s, sp, sps, iv,
    acc, rbuf, pbuf, pout, s1, ob1, ob2,
    ld, ldsem_out,
    g_send, g_recv, a_send, a_recv, c_send, c_recv,
    i_send, i_recv, x_send, x_recv, k_send, k_recv, p_send, p_recv,
    nb_send, nb_recv, sx_send, sx_recv, sk_send, sk_recv,
):
    leaf = lax.axis_index("leaf")
    g = lax.axis_index("grid")
    z, y = leaf // NY, leaf % NY
    x, c = g // 2, g % 2
    sib = (leaf, x * 2 + (1 - c))

    def at_x(xx):
        return (leaf, xx * 2 + c)

    def rcopy(src, dst, ssem, rsem, dev):
        return pltpu.make_async_remote_copy(
            src_ref=src, dst_ref=dst, send_sem=ssem, recv_sem=rsem, device_id=dev, device_id_type=MESH
        )

    def same(ref, ssem, rsem, dev):
        return rcopy(ref, ref, ssem, rsem, dev)

    own_rows = topb.at[pl.ds(pl.multiple_of(g * 16, 16), 16), :]
    half = pl.ds(pl.multiple_of(jnp.where(x >= 2, H, 0), H), H)
    loads = [
        (top, own_rows),
        (upd1.at[0], u1),
        (rows1, t1s),
        (right1.at[0], r1),
        (inv1.at[0, half], iv.at[ONE, :, pl.ds(0, B)]),
        (rows2, t2s),
        (upd2, u2),
        (seps, sps),
        (right2, r2),
        (inv2.at[:, half], iv.at[pl.ds(0, C2), :, pl.ds(0, B)]),
    ]
    loads += [(rows1.at[:, pl.ds(d * BD, BD)], t1.at[d]) for d in range(U // BD)]
    loads += [(rows2.at[:, pl.ds(d * BD, BD)], t2.at[d]) for d in range(UT // BD)]
    loads += [(seps.at[:, pl.ds(d * BD, BD)], sp.at[d]) for d in range(UP // BD)]
    loads = [pltpu.make_async_copy(a, b, ld.at[i]) for i, (a, b) in enumerate(loads)]
    for copy in loads:
        copy.start()

    barrier = pltpu.get_barrier_semaphore()

    def greet(dev):
        pl.semaphore_signal(barrier, inc=1, device_id=dev, device_id_type=MESH)

    for d in range(1, 8):
        greet((leaf, (g + d) % 8))
    for d in range(1, NY):
        greet((z * NY + (y + d) % NY, g))
    for d in range(1, NZ):
        greet((((z + d) % NZ) * NY + y, g))

    @pl.when(leaf > 0)
    def _():
        greet((leaf - 1, g))

    @pl.when(leaf < LEAVES - 1)
    def _():
        greet((leaf + 1, g))

    @pl.when(x == 1)
    def _():
        def zero(f, carry):
            for k in range(2):
                rbuf[f, k] = jnp.zeros((R, B), BF)
            return carry

        lax.fori_loop(0, C2 + 1, zero, 0)

    ends = jnp.where(leaf > 0, 1, 0) + jnp.where(leaf < LEAVES - 1, 1, 0)
    pl.semaphore_wait(barrier, 7 + (NY - 1) + (NZ - 1) + ends)

    loads[0].wait()
    for d in range(1, 8):
        rcopy(own_rows, own_rows, g_send.at[d - 1], g_recv.at[d - 1], (leaf, (g + d) % 8)).start()
    def ship(f):
        src = inv1.at[0, pl.ds(H, H)] if f is ONE else inv2.at[f, pl.ds(H, H)]
        return rcopy(src, iv.at[f, :, pl.ds(B, B)], i_send.at[f], i_recv.at[f], at_x(3 - x))

    def each_front(action):
        def one(f, carry):
            action(f)
            return carry

        lax.fori_loop(0, C2, one, 0)

    @pl.when(x < 2)
    def _():
        ship(ONE).start()
        each_front(lambda f: ship(f).start())

    for d in range(1, 8):
        other = (g + 8 - d) % 8
        part = topb.at[pl.ds(pl.multiple_of(other * 16, 16), 16), :]
        same(part, g_send.at[d - 1], g_recv.at[d - 1], (leaf, other)).wait_recv()
    block = topb[...].astype(F32).T.astype(BF)
    topT[z, y // 2, y % 2] = block.reshape(2, 128, B)

    def yz(zz, yy):
        return (((zz + NZ) % NZ) * NY + (yy + NY) % NY, g)

    def hand(region, i):
        same(region, c_send.at[i], c_recv.at[i], sib).start()

    def block_at(zz, yy, core):
        zz, yy = (zz + NZ) % NZ, (yy + NY) % NY
        return topT.at[zz, yy // 2, yy % 2, core]

    def plane(zz):
        return topT.at[(zz + NZ) % NZ, :, :, 0]

    def half_plane(zz, i):
        return topT.at[(zz + NZ) % NZ, i, :, 0]

    def column(yy):
        yy = (yy + NY) % NY
        return topT.at[:, yy // 2, yy % 2, 1]

    def pieces0():
        out = [block_at(z, y - d, 0) for d in (1, 3, 2)]
        out += [plane(z - 1), plane(z + 1), plane(z - 2), plane(z + 2)]
        return out + [plane(z - 3), plane(z + 3), half_plane(z - 4, 0), half_plane(z + 4, 1)]

    def pieces1():
        return [block_at(z - i, y, 1) for i in range(1, NZ)] + [column(y - d) for d in (1, 3, 2)]

    def send(region, i, dev):
        same(region, a_send.at[i], a_recv.at[i], dev).start()

    def gone(got, other):
        for i, region in enumerate(got):
            same(region, a_send.at[i], a_recv.at[i], sib).wait_send()
            same(region, c_send.at[i], c_recv.at[i], sib).wait_send()
        for i, region in enumerate(other):
            same(region, c_send.at[i], c_recv.at[i], sib).wait_recv()

    @pl.when(c == 0)
    def _():
        got = pieces0()

        def arrived(i):
            same(got[i], a_send.at[i], a_recv.at[i], sib).wait_recv()

        for i, d in enumerate((1, 3, 2)):
            send(block_at(z, y, 0), i, yz(z, y + d))
        for i in range(3):
            arrived(i)
        for i, d in ((5, 2), (6, -2), (3, 1), (4, -1)):
            send(plane(z), i, yz(z + d, y))
        for i in range(3):
            hand(got[i], i)
        for i in (3, 4):
            arrived(i)
            hand(got[i], i)
        arrived(5)
        send(plane(z - 2), 7, yz(z + 1, y))
        send(half_plane(z - 2, 0), 9, yz(z + 2, y))
        arrived(6)
        send(plane(z + 2), 8, yz(z - 1, y))
        send(half_plane(z + 2, 1), 10, yz(z - 2, y))
        for i in (5, 6):
            hand(got[i], i)
        for i in (7, 8, 9, 10):
            arrived(i)
            hand(got[i], i)
        gone(got, pieces1())

    @pl.when(c == 1)
    def _():
        got = pieces1()

        def arrived(i):
            same(got[i], a_send.at[i], a_recv.at[i], sib).wait_recv()

        for i in (4, 3, 5, 2, 6, 1, 7):
            send(block_at(z, y, 1), i - 1, yz(z + i, y))
        for i in range(7):
            arrived(i)
        for i, d in ((9, 2), (7, 1), (8, 3)):
            send(column(y), i, yz(z, y + d))
        for i in range(7):
            hand(got[i], i)
        for i in (7, 8, 9):
            arrived(i)
            hand(got[i], i)
        gone(got, pieces0())

    for copy in loads[1:]:
        copy.wait()

    def picked_product(count, pool, front, vec, sca, source, factor):
        nd, ns = count // BD, pool // BS
        total = jnp.zeros((R, B), F32)
        firsts = [sca[front, i * BD] for i in range(1, nd)]
        passed_at = []
        for i, v in enumerate(firsts):
            ends = jnp.int32(i)
            for j in range(1, ns):
                ends = ends + jnp.where(v >= j * BS, 1, 0)
            passed_at.append(ends)
        iota = lax.broadcasted_iota(jnp.int32, (BS, BD), 0)
        steps = nd + ns - 1
        pending = []
        for t in range(steps):
            d = jnp.int32(0)
            for ends in passed_at:
                d = d + jnp.where(ends < t, 1, 0)
            s = t - d
            picks = vec[d, pl.ds(front, 1), :]
            onehot = jnp.where(iota == picks - s * BS, 1.0, 0.0).astype(BF)
            got = jnp.dot(source(s), onehot, preferred_element_type=F32).astype(BF)
            pending.append((got, d))
            while len(pending) > (DELAY if t < steps - 1 else 0):
                got, d = pending.pop(0)
                total = total + jnp.dot(got, factor(d), preferred_element_type=F32)
        return total

    def top_rows(s):
        pair = topT[s >> 1, s & 1]
        return jnp.concatenate([pair[i].reshape(R, B) for i in range(2)], axis=1)

    twin = jnp.where(x >= 2, 5 - x, jnp.where(x == 1, 0, 1))
    sends, gets = x >= 1, x != 1

    def xs(f, k, dest):
        return same(rbuf.at[f, 2 * k + c], x_send.at[f], x_recv.at[f], at_x(dest))

    def ks(f, i, k, core):
        return same(rbuf.at[f, 2 * k + core], k_send.at[f, i], k_recv.at[f, i], sib)

    def ps(f):
        return rcopy(pout.at[f], pbuf.at[f], p_send.at[f], p_recv.at[f], at_x(3 - x))

    def own_sends(f):
        @pl.when(sends)
        def _():
            xs(f, x, twin).start()

        ks(f, 0, x, c).start()

    def first_hop(f):
        @pl.when(gets)
        def _():
            xs(f, twin, twin).wait_recv()
            ks(f, 1, twin, c).start()

    def from_core(f):
        ks(f, 0, x, 1 - c).wait_recv()

        @pl.when(gets)
        def _():
            ks(f, 1, twin, 1 - c).wait_recv()

    lanes = lax.broadcasted_iota(jnp.int32, (R, B), 1) + g * B

    def upper(f, live, out):
        from_core(f)
        if f is ONE:
            ship(ONE).wait_recv()
        else:
            ship(f).wait_recv()
        lhs = jnp.concatenate([rbuf[f, 4 + k] for k in range(4)], axis=1)
        both = jnp.dot(lhs, iv[f], preferred_element_type=F32)
        pout[f] = both[:, B:].astype(BF)
        ps(f).start()
        out(jnp.where(lanes < live, both[:, :B], 0.0))

    def lower(f, live, out):
        from_core(f)
        lhs = jnp.concatenate([rbuf[f, k] for k in range(4)], axis=1)
        own = jnp.dot(lhs, iv[f, :, :B], preferred_element_type=F32)
        ps(f).wait_recv()
        out(jnp.where(lanes < live, own + pbuf[f].astype(F32), 0.0))

    total1 = picked_product(U, LEAVES * B, 0, t1, t1s, top_rows, lambda d: u1[d])
    rbuf[ONE, g] = (r1[...].astype(F32).T - total1).astype(BF)
    own_sends(ONE)

    def s1_x(slot, d):
        return same(s1.at[slot, g], sx_send.at[slot, d - 1], sx_recv.at[slot, d - 1], at_x((x + d) % NX))

    def s1_x_got(slot, d):
        return s1.at[slot, 2 * ((x + NX - d) % NX) + c]

    def s1_k(slot, k, core):
        return same(s1.at[slot, 2 * k + core], sk_send.at[slot, k], sk_recv.at[slot, k], sib)

    def with_slots(slots, body):
        for slot in slots:
            if slot == 1:
                body(slot)
            else:

                @pl.when((leaf > 0) if slot == 0 else (leaf < LEAVES - 1))
                def _():
                    body(slot)

    def s1_up():
        return rcopy(s1.at[1, g], s1.at[0, g], nb_send.at[0], nb_recv.at[0], (leaf + 1, g))

    def s1_down():
        return rcopy(s1.at[1, g], s1.at[2, g], nb_send.at[1], nb_recv.at[1], (leaf - 1, g))

    def out_one(solved):
        s1[1, g] = solved.astype(BF)

        @pl.when(leaf < LEAVES - 1)
        def _():
            s1_up().start()

        @pl.when(leaf > 0)
        def _():
            s1_down().start()

        spread(1)
        ob1[...] = solved.T.astype(BF)
        pltpu.make_async_copy(ob1, out1.at[0], ldsem_out.at[C2]).start()

    def spread(slot):
        def over_x():
            for d in (2, 1, 3):
                s1_x(slot, d).start()

        if slot == 1:
            over_x()
        else:
            pl.when(c == 0)(over_x)
        s1_k(slot, x, c).start()

    def s1_relay(d, act):
        k = 2 * ((x + NX - d) % NX) + c

        @pl.when(leaf < LEAVES - 1)
        def _():
            act(rcopy(s1.at[1, k], s1.at[0, k], sx_send.at[0, d - 1], sx_recv.at[0, d - 1], (leaf + 1, g)))

        @pl.when(leaf > 0)
        def _():
            act(rcopy(s1.at[1, k], s1.at[2, k], sx_send.at[2, d - 1], sx_recv.at[2, d - 1], (leaf - 1, g)))

    def s1_neighbours():
        def body(slot):
            if slot == 0:
                s1_up().wait_recv()
            else:
                s1_down().wait_recv()
            spread(slot)

        with_slots((0, 2), body)

    def s1_cross(slots):
        def body(slot):
            for d in (1, 3, 2):
                same(s1_x_got(slot, d), sx_send.at[slot, d - 1], sx_recv.at[slot, d - 1], sib).wait_recv()
                if slot == 1:
                    pl.when(c == 1)(lambda: s1_relay(d, lambda copy: copy.start()))
                s1_k(slot, (x + NX - d) % NX, c).start()

        with_slots(slots, body)

    def s1_end():
        def body(slot):
            for k in range(NX):
                s1_k(slot, k, 1 - c).wait_recv()

        with_slots((1, 0, 2), body)

    def top_part(f):
        acc[f] = picked_product(UT, LEAVES * B, f, t2, t2s, top_rows, lambda d: u2[f, d])

    def parent_part(f):
        slot = jnp.clip(parent_s[f] - leaf + 1, 0, 2)

        def parent_rows(s):
            return jnp.concatenate([s1[slot, 2 * s], s1[slot, 2 * s + 1]], axis=1)

        total = picked_product(UP, S, f, sp, sps, parent_rows, lambda d: u2[f, UT // BD + d])
        rbuf[f, g] = (r2[f].astype(F32).T - acc[f] - total).astype(BF)
        own_sends(f)

    def out_two(f):
        def out(solved):
            ob2[f] = solved.T.astype(BF)
            pltpu.make_async_copy(ob2.at[f], out2.at[f], ldsem_out.at[f]).start()

        return out

    def body(it, carry):
        pl.when(it == 1)(lambda: first_hop(ONE))
        pl.when(jnp.logical_and(it == 2, x >= 2))(lambda: upper(ONE, live1_s[0], out_one))
        pl.when(jnp.logical_and(it == 3, x < 2))(lambda: lower(ONE, live1_s[0], out_one))

        @pl.when(jnp.logical_and(it == 4, c == 0))
        def _():
            s1_neighbours()
            s1_cross((1,))

        @pl.when(jnp.logical_and(it == 4, c == 1))
        def _():
            s1_cross((1,))
            s1_neighbours()

        pl.when(it == 5)(lambda: s1_cross((0, 2)))
        pl.when(it == 6)(s1_end)

        def staged(lag, action):
            @pl.when(jnp.logical_and(it >= lag, it < C2 + lag))
            def _():
                action(it - lag)

        def two_upper(f):
            pl.when(x >= 2)(lambda: upper(f, live2_s[f], out_two(f)))

        def two_lower(f):
            pl.when(x < 2)(lambda: lower(f, live2_s[f], out_two(f)))

        staged(LAG_C, first_hop)
        staged(LAG_D, two_upper)
        staged(LAG_B, parent_part)
        staged(LAG_E, two_lower)
        @pl.when(it < C2 // 2)
        def _():
            top_part(2 * it)
            top_part(2 * it + 1)

        return carry

    lax.fori_loop(0, C2 + LAG_E, body, 0)

    for d in range(1, 8):
        rcopy(own_rows, own_rows, g_send.at[d - 1], g_recv.at[d - 1], (leaf, (g + d) % 8)).wait_send()

    def finish(f, carry):
        ks(f, 0, x, c).wait_send()

        @pl.when(sends)
        def _():
            xs(f, x, twin).wait_send()

        @pl.when(gets)
        def _():
            ks(f, 1, twin, c).wait_send()

        @pl.when(x >= 2)
        def _():
            ps(f).wait_send()

        return carry

    lax.fori_loop(0, C2 + 1, finish, 0)

    @pl.when(x < 2)
    def _():
        ship(ONE).wait_send()
        each_front(lambda f: ship(f).wait_send())

    def finish_slot(slot):
        def over_x():
            for d in range(1, 4):
                s1_x(slot, d).wait_send()

        if slot == 1:
            over_x()
        else:
            pl.when(c == 0)(over_x)
        for k in range(NX):
            s1_k(slot, k, c).wait_send()

    @pl.when(c == 1)
    def _():
        for d in range(1, 4):
            s1_relay(d, lambda copy: copy.wait_send())

    with_slots((0, 1, 2), finish_slot)

    @pl.when(leaf < LEAVES - 1)
    def _():
        s1_up().wait_send()

    @pl.when(leaf > 0)
    def _():
        s1_down().wait_send()

    pltpu.make_async_copy(ob1, out1.at[0], ldsem_out.at[C2]).wait()

    def finish_out(f, carry):
        pltpu.make_async_copy(ob2.at[f], out2.at[f], ldsem_out.at[f]).wait()
        return carry

    lax.fori_loop(0, C2, finish_out, 0)


def local(
    top_solution, right_one, update_one, inverse_one, top_rows_one, live_one,
    right_two, update_two, inverse_two, top_rows_two, sep_rows, parent, live_two,
):
    anywhere = pl.BlockSpec(memory_space=pl.ANY)
    scalar = pl.BlockSpec(memory_space=pltpu.SMEM)
    dma = pltpu.SemaphoreType.DMA
    vm = pltpu.VMEM
    return pl.pallas_call(
        kernel,
        out_shape=(
            jax.ShapeDtypeStruct((1, B, R), BF),
            jax.ShapeDtypeStruct((C2, B, R), BF),
        ),
        in_specs=[anywhere] * 10 + [scalar] * 3,
        out_specs=(anywhere, anywhere),
        scratch_shapes=[
            vm((B, R), BF),
            vm((NZ, 2, 2, 2, 128, B), BF),
            vm((U // BD, BD, B), BF),
            vm((B, R), BF),
            vm((U // BD, 1, BD), jnp.int32),
            pltpu.SMEM((1, U), jnp.int32),
            vm((C2, U // BD, BD, B), BF),
            vm((C2, B, R), BF),
            vm((UT // BD, C2, BD), jnp.int32),
            pltpu.SMEM((C2, UT), jnp.int32),
            vm((UP // BD, C2, BD), jnp.int32),
            pltpu.SMEM((C2, UP), jnp.int32),
            vm((C2 + 1, H, 2 * B), BF),
            vm((C2, R, B), F32),
            vm((C2 + 1, 8, R, B), BF),
            vm((C2 + 1, R, B), BF),
            vm((C2 + 1, R, B), BF),
            vm((3, 8, R, B), BF),
            vm((B, R), BF),
            vm((C2, B, R), BF),
            dma((26,)), dma((C2 + 1,)),
            dma((7,)), dma((7,)), dma((11,)), dma((11,)), dma((11,)), dma((11,)),
            dma((C2 + 1,)), dma((C2 + 1,)), dma((C2 + 1,)), dma((C2 + 1,)), dma((C2 + 1, 2)), dma((C2 + 1, 2)),
            dma((C2 + 1,)), dma((C2 + 1,)),
            dma((2,)), dma((2,)), dma((3, 3)), dma((3, 3)), dma((3, 4)), dma((3, 4)),
        ],
        compiler_params=pltpu.CompilerParams(
            collective_id=0, has_side_effects=True, vmem_limit_bytes=56 * 1024 * 1024
        ),
        cost_estimate=pl.CostEstimate(flops=20_000_000_000, bytes_accessed=12_000_000, transcendentals=0),
        name="adjoint_solve",
    )(
        top_solution, right_one, update_one.reshape(1, U // BD, BD, B), inverse_one, top_rows_one,
        right_two, update_two.reshape(C2, U // BD, BD, B), inverse_two, top_rows_two, sep_rows,
        parent, live_one, live_two,
    )


def solution(mesh):
    in_specs = (
        P(("leaf", "grid"), None),
        P("leaf", "grid", None),
        P("leaf", None, "grid"),
        P("leaf", None, "grid"),
        P("leaf", None),
        P("leaf"),
        P("leaf", "grid", None),
        P("leaf", None, "grid"),
        P("leaf", None, "grid"),
        P("leaf", None),
        P("leaf", None),
        P("leaf"),
        P("leaf"),
    )
    out_specs = (P("leaf", "grid", None), P("leaf", "grid", None))
    return jax.shard_map(local, mesh=mesh, in_specs=in_specs, out_specs=out_specs, check_vma=False)
```

```python
import functools

import jax
import jax.numpy as jnp
from jax import lax
from jax.experimental import pallas as pl
from jax.experimental.pallas import tpu as pltpu
from jax.sharding import PartitionSpec as P

MESH = pl.DeviceIdType.MESH
F32 = jnp.float32
BF = jnp.bfloat16

R = 256
B = 128
S = 1024
U = 2048
UT = 1536
UP = 512
C2 = 12
NX, NY, NZ = 4, 4, 8
LEAVES = NY * NZ
BS = 256
DELAY = 3
BD = 256

ONE = C2
H = S // 2
LAG_B, LAG_C, LAG_D, LAG_E = 11, 15, 16, 19


def kernel(
    top, right1, upd1, inv1, rows1, right2, upd2, inv2, rows2, seps, live1, parent_s, live2_s,
    out1, out2,
    topb, topT, u1, r1, t1, t1s, u2, r2, t2, t2s, sp, sps, iv, i1, live1_s,
    acc, rbuf, pbuf, pout, s1, ob1, ob2,
    ld, ldsem_out,
    g_send, g_recv, a_send, a_recv, c_send, c_recv,
    i_send, i_recv, x_send, x_recv, k_send, k_recv, p_send, p_recv,
    o_send, o_recv, ok_send, ok_recv,
    nb_send, nb_recv, sx_send, sx_recv, sk_send, sk_recv,
):
    leaf = lax.axis_index("leaf")
    g = lax.axis_index("grid")
    z, y = leaf // NY, leaf % NY
    x, c = g // 2, g % 2
    sib = (leaf, x * 2 + (1 - c))

    def at_x(xx):
        return (leaf, xx * 2 + c)

    def rcopy(src, dst, ssem, rsem, dev):
        return pltpu.make_async_remote_copy(
            src_ref=src, dst_ref=dst, send_sem=ssem, recv_sem=rsem, device_id=dev, device_id_type=MESH
        )

    def same(ref, ssem, rsem, dev):
        return rcopy(ref, ref, ssem, rsem, dev)

    own_rows = topb.at[pl.ds(pl.multiple_of(g * 16, 16), 16), :]
    half = pl.ds(pl.multiple_of(jnp.where(x >= 2, H, 0), H), H)
    loads = [
        (top, own_rows),
        (upd1.at[0], u1),
        (rows1, t1s),
        (right1.at[0], r1),
        (inv1.at[0], i1),
        (live1, live1_s),
        (rows2, t2s),
        (upd2, u2),
        (seps, sps),
        (right2, r2),
        (inv2.at[:, half], iv.at[:, :, pl.ds(0, B)]),
    ]
    loads += [(rows1.at[:, pl.ds(d * BD, BD)], t1.at[d]) for d in range(U // BD)]
    loads += [(rows2.at[:, pl.ds(d * BD, BD)], t2.at[d]) for d in range(UT // BD)]
    loads += [(seps.at[:, pl.ds(d * BD, BD)], sp.at[d]) for d in range(UP // BD)]
    loads = [pltpu.make_async_copy(a, b, ld.at[i]) for i, (a, b) in enumerate(loads)]
    for copy in loads:
        copy.start()

    barrier = pltpu.get_barrier_semaphore()

    def greet(dev):
        pl.semaphore_signal(barrier, inc=1, device_id=dev, device_id_type=MESH)

    for d in range(1, 8):
        greet((leaf, (g + d) % 8))
    for d in range(1, NY):
        greet((z * NY + (y + d) % NY, g))
    for d in range(1, NZ):
        greet((((z + d) % NZ) * NY + y, g))

    @pl.when(leaf > 0)
    def _():
        greet((leaf - 1, g))

    @pl.when(leaf < LEAVES - 1)
    def _():
        greet((leaf + 1, g))

    @pl.when(x == 1)
    def _():
        def zero(f, carry):
            for k in range(2):
                rbuf[f, k] = jnp.zeros((R, B), BF)
            return carry

        lax.fori_loop(0, C2, zero, 0)

    for k in range(6):

        @pl.when(k < 2 * x)
        def _():
            rbuf[ONE, k] = jnp.zeros((R, B), BF)

    ends = jnp.where(leaf > 0, 1, 0) + jnp.where(leaf < LEAVES - 1, 1, 0)
    pl.semaphore_wait(barrier, 7 + (NY - 1) + (NZ - 1) + ends)

    loads[0].wait()
    for d in range(1, 8):
        rcopy(own_rows, own_rows, g_send.at[d - 1], g_recv.at[d - 1], (leaf, (g + d) % 8)).start()
    def ship(f):
        src = inv2.at[f, pl.ds(H, H)]
        return rcopy(src, iv.at[f, :, pl.ds(B, B)], i_send.at[f], i_recv.at[f], at_x(3 - x))

    def each_front(action):
        def one(f, carry):
            action(f)
            return carry

        lax.fori_loop(0, C2, one, 0)

    @pl.when(x < 2)
    def _():
        each_front(lambda f: ship(f).start())

    for d in range(1, 8):
        other = (g + 8 - d) % 8
        part = topb.at[pl.ds(pl.multiple_of(other * 16, 16), 16), :]
        same(part, g_send.at[d - 1], g_recv.at[d - 1], (leaf, other)).wait_recv()
    block = topb[...].astype(F32).T.astype(BF)
    topT[z, y // 2, y % 2] = block.reshape(2, 128, B)

    def yz(zz, yy):
        return (((zz + NZ) % NZ) * NY + (yy + NY) % NY, g)

    def hand(region, i):
        same(region, c_send.at[i], c_recv.at[i], sib).start()

    def block_at(zz, yy, core):
        zz, yy = (zz + NZ) % NZ, (yy + NY) % NY
        return topT.at[zz, yy // 2, yy % 2, core]

    def plane(zz):
        return topT.at[(zz + NZ) % NZ, :, :, 0]

    def half_plane(zz, i):
        return topT.at[(zz + NZ) % NZ, i, :, 0]

    def column(yy):
        yy = (yy + NY) % NY
        return topT.at[:, yy // 2, yy % 2, 1]

    def pieces0():
        out = [block_at(z, y - d, 0) for d in (1, 3, 2)]
        out += [plane(z - 1), plane(z + 1), plane(z - 2), plane(z + 2)]
        return out + [plane(z - 3), plane(z + 3), half_plane(z - 4, 0), half_plane(z + 4, 1)]

    def pieces1():
        return [block_at(z - i, y, 1) for i in range(1, NZ)] + [column(y - d) for d in (1, 3, 2)]

    def send(region, i, dev):
        same(region, a_send.at[i], a_recv.at[i], dev).start()

    def gone(got, other):
        for i, region in enumerate(got):
            same(region, a_send.at[i], a_recv.at[i], sib).wait_send()
            same(region, c_send.at[i], c_recv.at[i], sib).wait_send()
        for i, region in enumerate(other):
            same(region, c_send.at[i], c_recv.at[i], sib).wait_recv()

    @pl.when(c == 0)
    def _():
        got = pieces0()

        def arrived(i):
            same(got[i], a_send.at[i], a_recv.at[i], sib).wait_recv()

        for i, d in enumerate((1, 3, 2)):
            send(block_at(z, y, 0), i, yz(z, y + d))
        for i in range(3):
            arrived(i)
        for i, d in ((5, 2), (6, -2), (3, 1), (4, -1)):
            send(plane(z), i, yz(z + d, y))
        for i in range(3):
            hand(got[i], i)
        arrived(5)
        send(plane(z - 2), 7, yz(z + 1, y))
        send(half_plane(z - 2, 0), 9, yz(z + 2, y))
        arrived(6)
        send(plane(z + 2), 8, yz(z - 1, y))
        send(half_plane(z + 2, 1), 10, yz(z - 2, y))
        for i in (3, 4):
            arrived(i)
            hand(got[i], i)
        for i in (5, 6):
            hand(got[i], i)
        for i in (7, 8, 9, 10):
            arrived(i)
            hand(got[i], i)
        gone(got, pieces1())

    @pl.when(c == 1)
    def _():
        got = pieces1()

        def arrived(i):
            same(got[i], a_send.at[i], a_recv.at[i], sib).wait_recv()

        for i in (4, 3, 5, 2, 6, 1, 7):
            send(block_at(z, y, 1), i - 1, yz(z + i, y))
        for i in range(7):
            arrived(i)
        for i, d in ((9, 2), (7, 1), (8, 3)):
            send(column(y), i, yz(z, y + d))
        for i in range(7):
            hand(got[i], i)
        for i in (7, 8, 9):
            arrived(i)
            hand(got[i], i)
        gone(got, pieces0())

    for copy in loads[1:]:
        copy.wait()

    def picked_product(count, pool, front, vec, sca, source, factor):
        nd, ns = count // BD, pool // BS
        total = jnp.zeros((R, B), F32)
        firsts = [sca[front, i * BD] for i in range(1, nd)]
        passed_at = []
        for i, v in enumerate(firsts):
            ends = jnp.int32(i)
            for j in range(1, ns):
                ends = ends + jnp.where(v >= j * BS, 1, 0)
            passed_at.append(ends)
        iota = lax.broadcasted_iota(jnp.int32, (BS, BD), 0)
        steps = nd + ns - 1
        pending = []
        for t in range(steps):
            d = jnp.int32(0)
            for ends in passed_at:
                d = d + jnp.where(ends < t, 1, 0)
            s = t - d
            picks = vec[d, pl.ds(front, 1), :]
            onehot = jnp.where(iota == picks - s * BS, 1.0, 0.0).astype(BF)
            got = jnp.dot(source(s), onehot, preferred_element_type=F32).astype(BF)
            pending.append((got, d))
            while len(pending) > (DELAY if t < steps - 1 else 0):
                got, d = pending.pop(0)
                total = total + jnp.dot(got, factor(d), preferred_element_type=F32)
        return total

    def top_rows(s):
        pair = topT[s >> 1, s & 1]
        return jnp.concatenate([pair[i].reshape(R, B) for i in range(2)], axis=1)

    twin = jnp.where(x >= 2, 5 - x, jnp.where(x == 1, 0, 1))
    sends, gets = x >= 1, x != 1

    def xs(f, k, dest):
        return same(rbuf.at[f, 2 * k + c], x_send.at[f], x_recv.at[f], at_x(dest))

    def ks(f, i, k, core):
        return same(rbuf.at[f, 2 * k + core], k_send.at[f, i], k_recv.at[f, i], sib)

    def ps(f):
        return rcopy(pout.at[f], pbuf.at[f], p_send.at[f], p_recv.at[f], at_x(3 - x))

    def own_sends(f):
        @pl.when(sends)
        def _():
            xs(f, x, twin).start()

        ks(f, 0, x, c).start()

    def first_hop(f):
        @pl.when(gets)
        def _():
            xs(f, twin, twin).wait_recv()
            ks(f, 1, twin, c).start()

    def from_core(f):
        ks(f, 0, x, 1 - c).wait_recv()

        @pl.when(gets)
        def _():
            ks(f, 1, twin, 1 - c).wait_recv()

    lanes = lax.broadcasted_iota(jnp.int32, (R, B), 1) + g * B

    def upper(f, live, out):
        from_core(f)
        ship(f).wait_recv()
        lhs = jnp.concatenate([rbuf[f, 4 + k] for k in range(4)], axis=1)
        both = jnp.dot(lhs, iv[f], preferred_element_type=F32)
        pout[f] = both[:, B:].astype(BF)
        ps(f).start()
        out(jnp.where(lanes < live, both[:, :B], 0.0))

    def lower(f, live, out):
        from_core(f)
        lhs = jnp.concatenate([rbuf[f, k] for k in range(4)], axis=1)
        own = jnp.dot(lhs, iv[f, :, :B], preferred_element_type=F32)
        ps(f).wait_recv()
        out(jnp.where(lanes < live, own + pbuf[f].astype(F32), 0.0))

    total1 = picked_product(U, LEAVES * B, 0, t1, t1s, top_rows, lambda d: u1[d])
    rbuf[ONE, g] = (r1[...].astype(F32).T - total1).astype(BF)

    def o_x(k, dest):
        return same(rbuf.at[ONE, 2 * k + c], o_send.at[dest], o_recv.at[k - 1], at_x(dest))

    def o_k(k, core):
        return same(rbuf.at[ONE, 2 * k + core], ok_send.at[k - 1], ok_recv.at[k - 1], sib)

    def one_sends(act):
        for dest in range(3):
            pl.when(dest < x)(lambda: act(o_x(x, dest)))
        act(ks(ONE, 0, x, c))

    def one_first_hop():
        for k in range(1, 4):

            @pl.when(k > x)
            def _():
                o_x(k, 0).wait_recv()
                o_k(k, c).start()

    def solve_one():
        ks(ONE, 0, x, 1 - c).wait_recv()
        for k in range(1, 4):
            pl.when(k > x)(lambda: o_k(k, 1 - c).wait_recv())
        lhs = jnp.concatenate([rbuf[ONE, k] for k in range(8)], axis=1)
        solved = jnp.dot(lhs, i1[...], preferred_element_type=F32)
        out_one(jnp.where(lanes < live1_s[0], solved, 0.0))

    one_sends(lambda copy: copy.start())

    def s1_x(slot, d):
        return same(s1.at[slot, g], sx_send.at[slot, d - 1], sx_recv.at[slot, d - 1], at_x((x + d) % NX))

    def s1_x_got(slot, d):
        return s1.at[slot, 2 * ((x + NX - d) % NX) + c]

    def s1_k(slot, k, core):
        return same(s1.at[slot, 2 * k + core], sk_send.at[slot, k], sk_recv.at[slot, k], sib)

    def with_slots(slots, body):
        for slot in slots:
            if slot == 1:
                body(slot)
            else:

                @pl.when((leaf > 0) if slot == 0 else (leaf < LEAVES - 1))
                def _():
                    body(slot)

    def s1_up():
        return rcopy(s1.at[1, g], s1.at[0, g], nb_send.at[0], nb_recv.at[0], (leaf + 1, g))

    def s1_down():
        return rcopy(s1.at[1, g], s1.at[2, g], nb_send.at[1], nb_recv.at[1], (leaf - 1, g))

    def out_one(solved):
        s1[1, g] = solved.astype(BF)

        @pl.when(leaf < LEAVES - 1)
        def _():
            s1_up().start()

        @pl.when(leaf > 0)
        def _():
            s1_down().start()

        spread(1)
        ob1[...] = solved.T.astype(BF)
        pltpu.make_async_copy(ob1, out1.at[0], ldsem_out.at[C2]).start()

    def spread(slot):
        def over_x():
            for d in (2, 1, 3):
                s1_x(slot, d).start()

        if slot == 1:
            over_x()
        else:
            pl.when(c == 0)(over_x)
        s1_k(slot, x, c).start()

    def s1_relay(d, act):
        k = 2 * ((x + NX - d) % NX) + c

        @pl.when(leaf < LEAVES - 1)
        def _():
            act(rcopy(s1.at[1, k], s1.at[0, k], sx_send.at[0, d - 1], sx_recv.at[0, d - 1], (leaf + 1, g)))

        @pl.when(leaf > 0)
        def _():
            act(rcopy(s1.at[1, k], s1.at[2, k], sx_send.at[2, d - 1], sx_recv.at[2, d - 1], (leaf - 1, g)))

    def s1_neighbours():
        def body(slot):
            if slot == 0:
                s1_up().wait_recv()
            else:
                s1_down().wait_recv()
            spread(slot)

        with_slots((0, 2), body)

    def s1_cross(slots):
        def body(slot):
            for d in (1, 3, 2):
                same(s1_x_got(slot, d), sx_send.at[slot, d - 1], sx_recv.at[slot, d - 1], sib).wait_recv()
                if slot == 1:
                    pl.when(c == 1)(lambda: s1_relay(d, lambda copy: copy.start()))
                s1_k(slot, (x + NX - d) % NX, c).start()

        with_slots(slots, body)

    def s1_end():
        def body(slot):
            for k in range(NX):
                s1_k(slot, k, 1 - c).wait_recv()

        with_slots((1, 0, 2), body)

    def top_part(f):
        acc[f] = picked_product(UT, LEAVES * B, f, t2, t2s, top_rows, lambda d: u2[f, d])

    def parent_part(f):
        slot = jnp.clip(parent_s[f] - leaf + 1, 0, 2)

        def parent_rows(s):
            return jnp.concatenate([s1[slot, 2 * s], s1[slot, 2 * s + 1]], axis=1)

        total = picked_product(UP, S, f, sp, sps, parent_rows, lambda d: u2[f, UT // BD + d])
        rbuf[f, g] = (r2[f].astype(F32).T - acc[f] - total).astype(BF)
        own_sends(f)

    def out_two(f):
        def out(solved):
            ob2[f] = solved.T.astype(BF)
            pltpu.make_async_copy(ob2.at[f], out2.at[f], ldsem_out.at[f]).start()

        return out

    def body(it, carry):
        pl.when(it == 3)(one_first_hop)
        pl.when(it == 4)(solve_one)
        pl.when(it == 6)(s1_neighbours)
        pl.when(it == 7)(lambda: s1_cross((1,)))
        pl.when(it == 10)(lambda: s1_cross((0, 2)))
        pl.when(it == 11)(s1_end)

        def staged(lag, action):
            @pl.when(jnp.logical_and(it >= lag, it < C2 + lag))
            def _():
                action(it - lag)

        def two_upper(f):
            pl.when(x >= 2)(lambda: upper(f, live2_s[f], out_two(f)))

        def two_lower(f):
            pl.when(x < 2)(lambda: lower(f, live2_s[f], out_two(f)))

        staged(LAG_C, first_hop)
        staged(LAG_D, two_upper)
        staged(LAG_B, parent_part)
        staged(LAG_E, two_lower)
        staged(0, top_part)
        return carry

    lax.fori_loop(0, C2 + LAG_E, body, 0)

    for d in range(1, 8):
        rcopy(own_rows, own_rows, g_send.at[d - 1], g_recv.at[d - 1], (leaf, (g + d) % 8)).wait_send()

    def finish(f, carry):
        ks(f, 0, x, c).wait_send()

        @pl.when(sends)
        def _():
            xs(f, x, twin).wait_send()

        @pl.when(gets)
        def _():
            ks(f, 1, twin, c).wait_send()

        @pl.when(x >= 2)
        def _():
            ps(f).wait_send()

        return carry

    lax.fori_loop(0, C2, finish, 0)
    one_sends(lambda copy: copy.wait_send())
    for k in range(1, 4):
        pl.when(k > x)(lambda: o_k(k, c).wait_send())

    @pl.when(x < 2)
    def _():
        each_front(lambda f: ship(f).wait_send())

    def finish_slot(slot):
        def over_x():
            for d in range(1, 4):
                s1_x(slot, d).wait_send()

        if slot == 1:
            over_x()
        else:
            pl.when(c == 0)(over_x)
        for k in range(NX):
            s1_k(slot, k, c).wait_send()

    @pl.when(c == 1)
    def _():
        for d in range(1, 4):
            s1_relay(d, lambda copy: copy.wait_send())

    with_slots((0, 1, 2), finish_slot)

    @pl.when(leaf < LEAVES - 1)
    def _():
        s1_up().wait_send()

    @pl.when(leaf > 0)
    def _():
        s1_down().wait_send()

    pltpu.make_async_copy(ob1, out1.at[0], ldsem_out.at[C2]).wait()

    def finish_out(f, carry):
        pltpu.make_async_copy(ob2.at[f], out2.at[f], ldsem_out.at[f]).wait()
        return carry

    lax.fori_loop(0, C2, finish_out, 0)


PARTS = 6


def hand_out(first, second, out1, out2, held, sem_in, sem_out):
    step = C2 // PARTS

    def part(ref, i):
        return ref.at[pl.ds(i * step, step)]

    copies = [
        (
            pltpu.make_async_copy(part(second, i), part(held, i), sem_in.at[i]),
            pltpu.make_async_copy(part(held, i), part(out2, i), sem_out.at[i]),
        )
        for i in range(PARTS)
    ]
    last = held.at[pl.ds(C2, 1)]
    copies.append(
        (
            pltpu.make_async_copy(first, last, sem_in.at[PARTS]),
            pltpu.make_async_copy(last, out1, sem_out.at[PARTS]),
        )
    )
    for get, _ in copies:
        get.start()
    for get, put in copies:
        get.wait()
        put.start()
    for _, put in copies:
        put.wait()


def local(
    top_solution, right_one, update_one, inverse_one, top_rows_one, live_one,
    right_two, update_two, inverse_two, top_rows_two, sep_rows, parent, live_two,
):
    anywhere = pl.BlockSpec(memory_space=pl.ANY)
    scalar = pl.BlockSpec(memory_space=pltpu.SMEM)
    dma = pltpu.SemaphoreType.DMA
    vm = pltpu.VMEM
    first, second = pl.pallas_call(
        kernel,
        out_shape=(
            jax.ShapeDtypeStruct((1, B, R), BF),
            jax.ShapeDtypeStruct((C2, B, R), BF),
        ),
        in_specs=[anywhere] * 11 + [scalar] * 2,
        out_specs=(anywhere, anywhere),
        scratch_shapes=[
            vm((B, R), BF),
            vm((NZ, 2, 2, 2, 128, B), BF),
            vm((U // BD, BD, B), BF),
            vm((B, R), BF),
            vm((U // BD, 1, BD), jnp.int32),
            pltpu.SMEM((1, U), jnp.int32),
            vm((C2, U // BD, BD, B), BF),
            vm((C2, B, R), BF),
            vm((UT // BD, C2, BD), jnp.int32),
            pltpu.SMEM((C2, UT), jnp.int32),
            vm((UP // BD, C2, BD), jnp.int32),
            pltpu.SMEM((C2, UP), jnp.int32),
            vm((C2, H, 2 * B), BF),
            vm((S, B), BF),
            pltpu.SMEM((1,), jnp.int32),
            vm((C2, R, B), F32),
            vm((C2 + 1, 8, R, B), BF),
            vm((C2, R, B), BF),
            vm((C2, R, B), BF),
            vm((3, 8, R, B), BF),
            vm((B, R), BF),
            vm((C2, B, R), BF),
            dma((27,)), dma((C2 + 1,)),
            dma((7,)), dma((7,)), dma((11,)), dma((11,)), dma((11,)), dma((11,)),
            dma((C2,)), dma((C2,)), dma((C2,)), dma((C2,)), dma((C2 + 1, 2)), dma((C2 + 1, 2)),
            dma((C2,)), dma((C2,)),
            dma((3,)), dma((3,)), dma((3,)), dma((3,)),
            dma((2,)), dma((2,)), dma((3, 3)), dma((3, 3)), dma((3, 4)), dma((3, 4)),
        ],
        compiler_params=pltpu.CompilerParams(
            collective_id=0, has_side_effects=True, vmem_limit_bytes=56 * 1024 * 1024
        ),
        cost_estimate=pl.CostEstimate(flops=20_000_000_000, bytes_accessed=12_000_000, transcendentals=0),
        name="adjoint_solve",
    )(
        top_solution, right_one, update_one.reshape(1, U // BD, BD, B), inverse_one, top_rows_one,
        right_two, update_two.reshape(C2, U // BD, BD, B), inverse_two, top_rows_two, sep_rows,
        live_one, parent, live_two,
    )
    return pl.pallas_call(
        hand_out,
        out_shape=(
            jax.ShapeDtypeStruct((1, B, R), BF),
            jax.ShapeDtypeStruct((C2, B, R), BF),
        ),
        in_specs=[anywhere] * 2,
        out_specs=(anywhere, anywhere),
        scratch_shapes=[pltpu.VMEM((C2 + 1, B, R), BF), dma((PARTS + 1,)), dma((PARTS + 1,))],
        compiler_params=pltpu.CompilerParams(vmem_limit_bytes=56 * 1024 * 1024),
        name="hand_out",
    )(first, second)


def solution(mesh):
    in_specs = (
        P(("leaf", "grid"), None),
        P("leaf", "grid", None),
        P("leaf", None, "grid"),
        P("leaf", None, "grid"),
        P("leaf", None),
        P("leaf"),
        P("leaf", "grid", None),
        P("leaf", None, "grid"),
        P("leaf", None, "grid"),
        P("leaf", None),
        P("leaf", None),
        P("leaf"),
        P("leaf"),
    )
    out_specs = (P("leaf", "grid", None), P("leaf", "grid", None))
    return jax.shard_map(local, mesh=mesh, in_specs=in_specs, out_specs=out_specs, check_vma=False)
```

```python
import functools

import jax
import jax.numpy as jnp
from jax import lax
from jax.experimental import pallas as pl
from jax.experimental.pallas import tpu as pltpu
from jax.sharding import PartitionSpec as P

MESH = pl.DeviceIdType.MESH
F32 = jnp.float32
BF = jnp.bfloat16

R = 256
B = 128
S = 1024
U = 2048
UT = 1536
UP = 512
C2 = 12
NX, NY, NZ = 4, 4, 8
LEAVES = NY * NZ
BS = 256
BD = 256

ONE = C2
H = S // 2
W = 1
LAG_B, LAG_C, LAG_D, LAG_E = 12, 16, 17, 20


def kernel(
    top, right1, upd1, inv1, rows1, right2, upd2, inv2, rows2, seps, live1, parent_s, live2_s,
    out1, out2,
    topb, topT, u1, r1, t1, t1s, u2, r2, t2, t2s, sp, sps, iv, i1, live1_s,
    acc, cum, rbuf, pbuf, pout, s1, ob1, ob2,
    ld, ldsem_out,
    g_send, g_recv, a_send, a_recv, c_send, c_recv,
    i_send, i_recv, x_send, x_recv, k_send, k_recv, p_send, p_recv,
    o_send, o_recv, ok_send, ok_recv,
    nb_send, nb_recv, sx_send, sx_recv, sk_send, sk_recv,
):
    leaf = lax.axis_index("leaf")
    g = lax.axis_index("grid")
    z, y = leaf // NY, leaf % NY
    x, c = g // 2, g % 2
    sib = (leaf, x * 2 + (1 - c))

    def at_x(xx):
        return (leaf, xx * 2 + c)

    def rcopy(src, dst, ssem, rsem, dev):
        return pltpu.make_async_remote_copy(
            src_ref=src, dst_ref=dst, send_sem=ssem, recv_sem=rsem, device_id=dev, device_id_type=MESH
        )

    def same(ref, ssem, rsem, dev):
        return rcopy(ref, ref, ssem, rsem, dev)

    own_rows = topb.at[pl.ds(pl.multiple_of(g * 16, 16), 16), :]
    half = pl.ds(pl.multiple_of(jnp.where(x >= 2, H, 0), H), H)
    loads = [
        (top, own_rows),
        (upd1.at[0], u1),
        (rows1, t1s),
        (right1.at[0], r1),
        (inv1.at[0], i1),
        (live1, live1_s),
        (rows2, t2s),
        (upd2, u2),
        (seps, sps),
        (right2, r2),
        (inv2.at[:, half], iv.at[:, :, pl.ds(0, B)]),
    ]
    loads += [(rows1.at[:, pl.ds(d * BD, BD)], t1.at[d]) for d in range(U // BD)]
    loads += [(rows2.at[:, pl.ds(d * BD, BD)], t2.at[d]) for d in range(UT // BD)]
    loads += [(seps.at[:, pl.ds(d * BD, BD)], sp.at[d]) for d in range(UP // BD)]
    loads = [pltpu.make_async_copy(a, b, ld.at[i]) for i, (a, b) in enumerate(loads)]
    for copy in loads:
        copy.start()

    barrier = pltpu.get_barrier_semaphore()

    def greet(dev):
        pl.semaphore_signal(barrier, inc=1, device_id=dev, device_id_type=MESH)

    for d in range(1, 8):
        greet((leaf, (g + d) % 8))
    for d in range(1, NY):
        greet((z * NY + (y + d) % NY, g))
    for d in range(1, NZ):
        greet((((z + d) % NZ) * NY + y, g))

    @pl.when(leaf > 0)
    def _():
        greet((leaf - 1, g))

    @pl.when(leaf < LEAVES - 1)
    def _():
        greet((leaf + 1, g))

    @pl.when(x == 1)
    def _():
        def zero(f, carry):
            for k in range(2):
                rbuf[f, k] = jnp.zeros((R, B), BF)
            return carry

        lax.fori_loop(0, C2, zero, 0)

    for k in range(6):

        @pl.when(k < 2 * x)
        def _():
            rbuf[ONE, k] = jnp.zeros((R, B), BF)

    ends = jnp.where(leaf > 0, 1, 0) + jnp.where(leaf < LEAVES - 1, 1, 0)
    pl.semaphore_wait(barrier, 7 + (NY - 1) + (NZ - 1) + ends)

    loads[0].wait()
    for d in range(1, 8):
        rcopy(own_rows, own_rows, g_send.at[d - 1], g_recv.at[d - 1], (leaf, (g + d) % 8)).start()
    def ship(f):
        src = inv2.at[f, pl.ds(H, H)]
        return rcopy(src, iv.at[f, :, pl.ds(B, B)], i_send.at[f], i_recv.at[f], at_x(3 - x))

    def each_front(action):
        def one(f, carry):
            action(f)
            return carry

        lax.fori_loop(0, C2, one, 0)

    @pl.when(x < 2)
    def _():
        each_front(lambda f: ship(f).start())

    for d in range(1, 8):
        other = (g + 8 - d) % 8
        part = topb.at[pl.ds(pl.multiple_of(other * 16, 16), 16), :]
        same(part, g_send.at[d - 1], g_recv.at[d - 1], (leaf, other)).wait_recv()
    block = topb[...].astype(F32).T.astype(BF)
    topT[z, y // 2, y % 2] = block.reshape(2, 128, B)

    def yz(zz, yy):
        return (((zz + NZ) % NZ) * NY + (yy + NY) % NY, g)

    def hand(region, i):
        same(region, c_send.at[i], c_recv.at[i], sib).start()

    def block_at(zz, yy, core):
        zz, yy = (zz + NZ) % NZ, (yy + NY) % NY
        return topT.at[zz, yy // 2, yy % 2, core]

    def plane(zz):
        return topT.at[(zz + NZ) % NZ, :, :, 0]

    def half_plane(zz, i):
        return topT.at[(zz + NZ) % NZ, i, :, 0]

    def column(yy):
        yy = (yy + NY) % NY
        return topT.at[:, yy // 2, yy % 2, 1]

    def pieces0():
        out = [block_at(z, y - d, 0) for d in (1, 3, 2)]
        out += [plane(z - 1), plane(z + 1), plane(z - 2), plane(z + 2)]
        return out + [plane(z - 3), plane(z + 3), half_plane(z - 4, 0), half_plane(z + 4, 1)]

    def pieces1():
        return [block_at(z - i, y, 1) for i in range(1, NZ)] + [column(y - d) for d in (1, 3, 2)]

    def send(region, i, dev):
        same(region, a_send.at[i], a_recv.at[i], dev).start()

    def gone(got):
        for i, region in enumerate(got):
            same(region, a_send.at[i], a_recv.at[i], sib).wait_send()
            same(region, c_send.at[i], c_recv.at[i], sib).wait_send()

    def handed(other):
        for i, region in enumerate(other):
            same(region, c_send.at[i], c_recv.at[i], sib).wait_recv()

    def turn_right():
        for copy in loads[1:]:
            copy.wait()

        def one(f, carry):
            acc[f] = r2[f].astype(F32).T
            return carry

        lax.fori_loop(0, C2, one, 0)

    @pl.when(c == 0)
    def _():
        got = pieces0()

        def arrived(i):
            same(got[i], a_send.at[i], a_recv.at[i], sib).wait_recv()

        for i, d in enumerate((1, 3, 2)):
            send(block_at(z, y, 0), i, yz(z, y + d))
        turn_right()
        for i in range(3):
            arrived(i)
        for i, d in ((5, 2), (6, -2), (3, 1), (4, -1)):
            send(plane(z), i, yz(z + d, y))
        for i in range(3):
            hand(got[i], i)
        arrived(5)
        send(plane(z - 2), 7, yz(z + 1, y))
        send(half_plane(z - 2, 0), 9, yz(z + 2, y))
        arrived(6)
        send(plane(z + 2), 8, yz(z - 1, y))
        send(half_plane(z + 2, 1), 10, yz(z - 2, y))
        for i in (3, 4):
            arrived(i)
            hand(got[i], i)
        for i in (5, 6):
            hand(got[i], i)
        for i in (7, 8, 9, 10):
            arrived(i)
            hand(got[i], i)
        handed(pieces1())

    @pl.when(c == 1)
    def _():
        got = pieces1()

        def arrived(i):
            same(got[i], a_send.at[i], a_recv.at[i], sib).wait_recv()

        for i in (4, 3, 5, 2, 6, 1, 7):
            send(block_at(z, y, 1), i - 1, yz(z + i, y))
        turn_right()
        for i in range(7):
            arrived(i)
        for i, d in ((9, 2), (7, 1), (8, 3)):
            send(column(y), i, yz(z, y + d))
        for i in range(7):
            hand(got[i], i)
        for i in (7, 8, 9):
            arrived(i)
            hand(got[i], i)
        handed(pieces0())


    def picked_product(count, pool, front, vec, sca, source, factor):
        nd, ns = count // BD, pool // BS
        total = jnp.zeros((R, B), F32)
        firsts = [sca[front, i * BD] for i in range(1, nd)]
        passed_at = []
        for i, v in enumerate(firsts):
            ends = jnp.int32(i)
            for j in range(1, ns):
                ends = ends + jnp.where(v >= j * BS, 1, 0)
            passed_at.append(ends)
        iota = lax.broadcasted_iota(jnp.int16, (BS, BD), 0)
        steps = nd + ns - 1
        held = None
        for t in range(steps):
            d = jnp.int32(0)
            for ends in passed_at:
                d = d + jnp.where(ends < t, 1, 0)
            s = t - d
            picks = vec[d, pl.ds(front, 1), :]
            onehot = jnp.where(iota == (picks - s * BS).astype(jnp.int16), BF(1), BF(0))
            got = jnp.dot(source(s), onehot, preferred_element_type=F32).astype(BF)
            if t:
                keep = jnp.where(d == held[1], 1.0, 0.0)
                got = got + held[0] * jnp.full((R, BD), keep, F32).astype(BF)
            cum[t] = got
            held = (got, d)
        passed_at.append(steps - 1)
        for d, last in enumerate(passed_at):
            total = total + jnp.dot(cum[last], factor(d), preferred_element_type=F32)
        return total

    def top_rows(s):
        pair = topT[s >> 1, s & 1]
        return jnp.concatenate([pair[i].reshape(R, B) for i in range(2)], axis=1)

    twin = jnp.where(x >= 2, 5 - x, jnp.where(x == 1, 0, 1))
    sends, gets = x >= 1, x != 1

    def xs(f, k, dest):
        return same(rbuf.at[f, 2 * k + c], x_send.at[f], x_recv.at[f], at_x(dest))

    def ks(f, i, k, core):
        return same(rbuf.at[f, 2 * k + core], k_send.at[f, i], k_recv.at[f, i], sib)

    def ps(f):
        return rcopy(pout.at[f], pbuf.at[f], p_send.at[f], p_recv.at[f], at_x(3 - x))

    def own_sends(f):
        @pl.when(sends)
        def _():
            xs(f, x, twin).start()

        ks(f, 0, x, c).start()

    def first_hop(f):
        @pl.when(gets)
        def _():
            xs(f, twin, twin).wait_recv()
            ks(f, 1, twin, c).start()

    def from_core(f):
        ks(f, 0, x, 1 - c).wait_recv()

        @pl.when(gets)
        def _():
            ks(f, 1, twin, 1 - c).wait_recv()

    lanes = lax.broadcasted_iota(jnp.int32, (R, B), 1) + g * B

    def uppers(fronts, outs):
        for f in fronts:
            from_core(f)
            ship(f).wait_recv()
        both = []
        for f in fronts:
            lhs = jnp.concatenate([rbuf[f, 4 + k] for k in range(4)], axis=1)
            both.append(jnp.dot(lhs, iv[f], preferred_element_type=F32))
        for f, value in zip(fronts, both):
            pout[f] = value[:, B:].astype(BF)
        for f in fronts:
            ps(f).start()
        outs(fronts, [value[:, :B] for value in both])

    def lowers(fronts, outs):
        for f in fronts:
            from_core(f)
            ps(f).wait_recv()
        solved = []
        for f in fronts:
            lhs = jnp.concatenate([rbuf[f, k] for k in range(4)], axis=1)
            own = jnp.dot(lhs, iv[f, :, :B], preferred_element_type=F32)
            solved.append(own + pbuf[f].astype(F32))
        outs(fronts, solved)

    total1 = picked_product(U, LEAVES * B, 0, t1, t1s, top_rows, lambda d: u1[d])
    rbuf[ONE, g] = (r1[...].astype(F32).T - total1).astype(BF)

    def o_x(k, dest):
        return same(rbuf.at[ONE, 2 * k + c], o_send.at[dest], o_recv.at[k - 1], at_x(dest))

    def o_k(k, core):
        return same(rbuf.at[ONE, 2 * k + core], ok_send.at[k - 1], ok_recv.at[k - 1], sib)

    def one_sends(act):
        for dest in range(3):
            pl.when(dest < x)(lambda: act(o_x(x, dest)))
        act(ks(ONE, 0, x, c))

    def one_first_hop():
        for k in range(1, 4):

            @pl.when(k > x)
            def _():
                o_x(k, 0).wait_recv()
                o_k(k, c).start()

    def solve_one():
        ks(ONE, 0, x, 1 - c).wait_recv()
        for k in range(1, 4):
            pl.when(k > x)(lambda: o_k(k, 1 - c).wait_recv())
        lhs = jnp.concatenate([rbuf[ONE, k] for k in range(8)], axis=1)
        solved = jnp.dot(lhs, i1[...], preferred_element_type=F32)
        out_one(jnp.where(lanes < live1_s[0], solved, 0.0))

    one_sends(lambda copy: copy.start())

    def s1_x(slot, d):
        return same(s1.at[slot, g], sx_send.at[slot, d - 1], sx_recv.at[slot, d - 1], at_x((x + d) % NX))

    def s1_x_got(slot, d):
        return s1.at[slot, 2 * ((x + NX - d) % NX) + c]

    def s1_k(slot, k, core):
        return same(s1.at[slot, 2 * k + core], sk_send.at[slot, k], sk_recv.at[slot, k], sib)

    def with_slots(slots, body):
        for slot in slots:
            if slot == 1:
                body(slot)
            else:

                @pl.when((leaf > 0) if slot == 0 else (leaf < LEAVES - 1))
                def _():
                    body(slot)

    def s1_up():
        return rcopy(s1.at[1, g], s1.at[0, g], nb_send.at[0], nb_recv.at[0], (leaf + 1, g))

    def s1_down():
        return rcopy(s1.at[1, g], s1.at[2, g], nb_send.at[1], nb_recv.at[1], (leaf - 1, g))

    def out_one(solved):
        s1[1, g] = solved.astype(BF)

        @pl.when(leaf < LEAVES - 1)
        def _():
            s1_up().start()

        @pl.when(leaf > 0)
        def _():
            s1_down().start()

        spread(1)
        ob1[...] = solved.T.astype(BF)
        pltpu.make_async_copy(ob1, out1.at[0], ldsem_out.at[C2]).start()

    def spread(slot):
        def over_x():
            for d in (2, 1, 3):
                s1_x(slot, d).start()

        if slot == 1:
            over_x()
        else:
            pl.when(c == 0)(over_x)
        s1_k(slot, x, c).start()

    def s1_relay(d, act):
        k = 2 * ((x + NX - d) % NX) + c

        @pl.when(leaf < LEAVES - 1)
        def _():
            act(rcopy(s1.at[1, k], s1.at[0, k], sx_send.at[0, d - 1], sx_recv.at[0, d - 1], (leaf + 1, g)))

        @pl.when(leaf > 0)
        def _():
            act(rcopy(s1.at[1, k], s1.at[2, k], sx_send.at[2, d - 1], sx_recv.at[2, d - 1], (leaf - 1, g)))

    def s1_neighbours():
        def body(slot):
            if slot == 0:
                s1_up().wait_recv()
            else:
                s1_down().wait_recv()
            spread(slot)

        with_slots((0, 2), body)

    def s1_cross(slots):
        def body(slot):
            for d in (1, 3, 2):
                same(s1_x_got(slot, d), sx_send.at[slot, d - 1], sx_recv.at[slot, d - 1], sib).wait_recv()
                if slot == 1:
                    pl.when(c == 1)(lambda: s1_relay(d, lambda copy: copy.start()))
                s1_k(slot, (x + NX - d) % NX, c).start()

        with_slots(slots, body)

    def s1_end():
        def body(slot):
            for k in range(NX):
                s1_k(slot, k, 1 - c).wait_recv()

        with_slots((1, 0, 2), body)

    def top_part(f):
        acc[f] = acc[f] - picked_product(UT, LEAVES * B, f, t2, t2s, top_rows, lambda d: u2[f, d])

    def parent_parts(fronts):
        left = []
        for f in fronts:
            slot = jnp.clip(parent_s[f] - leaf + 1, 0, 2)

            def parent_rows(s, slot=slot):
                return jnp.concatenate([s1[slot, 2 * s], s1[slot, 2 * s + 1]], axis=1)

            total = picked_product(UP, S, f, sp, sps, parent_rows, lambda d, f=f: u2[f, UT // BD + d])
            left.append((acc[f] - total).astype(BF))
        for f, value in zip(fronts, left):
            rbuf[f, g] = value
        for f in fronts:
            own_sends(f)

    def out_two(fronts, solved):
        for f, value in zip(fronts, solved):
            ob2[f] = jnp.where(lanes < live2_s[f], value, 0.0).T.astype(BF)
        for f in fronts:
            pltpu.make_async_copy(ob2.at[f], out2.at[f], ldsem_out.at[f]).start()

    def finish(fronts):
        f, = fronts
        ks(f, 0, x, c).wait_send()

        @pl.when(sends)
        def _():
            xs(f, x, twin).wait_send()

        @pl.when(gets)
        def _():
            ks(f, 1, twin, c).wait_send()

        @pl.when(x >= 2)
        def _():
            ps(f).wait_send()


    def early_sends_gone():
        pl.when(c == 0)(lambda: gone(pieces0()))
        pl.when(c == 1)(lambda: gone(pieces1()))

    def later_sends_gone():
        for d in range(1, 8):
            rcopy(own_rows, own_rows, g_send.at[d - 1], g_recv.at[d - 1], (leaf, (g + d) % 8)).wait_send()

        one_sends(lambda copy: copy.wait_send())
        for k in range(1, 4):
            pl.when(k > x)(lambda: o_k(k, c).wait_send())

        @pl.when(x < 2)
        def _():
            each_front(lambda f: ship(f).wait_send())

        def finish_slot(slot):
            def over_x():
                for d in range(1, 4):
                    s1_x(slot, d).wait_send()

            if slot == 1:
                over_x()
            else:
                pl.when(c == 0)(over_x)
            for k in range(NX):
                s1_k(slot, k, c).wait_send()

        @pl.when(c == 1)
        def _():
            for d in range(1, 4):
                s1_relay(d, lambda copy: copy.wait_send())

        with_slots((0, 1, 2), finish_slot)

        @pl.when(leaf < LEAVES - 1)
        def _():
            s1_up().wait_send()

        @pl.when(leaf > 0)
        def _():
            s1_down().wait_send()


    def body(it, carry):
        pl.when(it == 3)(one_first_hop)
        pl.when(it == 4)(solve_one)
        pl.when(it == 7)(s1_neighbours)
        pl.when(it == 8)(lambda: s1_cross((1,)))
        pl.when(it == 11)(lambda: s1_cross((0, 2)))
        pl.when(it == 12)(s1_end)

        def staged(lag, action):
            @pl.when(jnp.logical_and(it >= lag, it < C2 // W + lag))
            def _():
                action([(it - lag) * W + i for i in range(W)])

        def first_hops(fronts):
            for f in fronts:
                first_hop(f)

        def two_upper(fronts):
            pl.when(x >= 2)(lambda: uppers(fronts, out_two))

        def two_lower(fronts):
            pl.when(x < 2)(lambda: lowers(fronts, out_two))

        staged(LAG_C, first_hops)
        staged(LAG_D, two_upper)
        staged(LAG_B, parent_parts)
        staged(LAG_E, two_lower)
        staged(LAG_E + 1, finish)
        pl.when(it == LAG_B + 2)(early_sends_gone)
        pl.when(it == LAG_C + 2)(later_sends_gone)
        pl.when(it < C2)(lambda: top_part(it))
        return carry

    lax.fori_loop(0, C2 + LAG_E + 1, body, 0)

    pltpu.make_async_copy(ob1, out1.at[0], ldsem_out.at[C2]).wait()

    def finish_out(f, carry):
        pltpu.make_async_copy(ob2.at[f], out2.at[f], ldsem_out.at[f]).wait()
        return carry

    lax.fori_loop(0, C2, finish_out, 0)


PARTS = 6


def hand_out(first, second, out1, out2, held, sem_in, sem_out):
    step = C2 // PARTS

    def part(ref, i):
        return ref.at[pl.ds(i * step, step)]

    copies = [
        (
            pltpu.make_async_copy(part(second, i), part(held, i), sem_in.at[i]),
            pltpu.make_async_copy(part(held, i), part(out2, i), sem_out.at[i]),
        )
        for i in range(PARTS)
    ]
    last = held.at[pl.ds(C2, 1)]
    copies.append(
        (
            pltpu.make_async_copy(first, last, sem_in.at[PARTS]),
            pltpu.make_async_copy(last, out1, sem_out.at[PARTS]),
        )
    )
    for get, _ in copies:
        get.start()
    for get, put in copies:
        get.wait()
        put.start()
    for _, put in copies:
        put.wait()


def local(
    top_solution, right_one, update_one, inverse_one, top_rows_one, live_one,
    right_two, update_two, inverse_two, top_rows_two, sep_rows, parent, live_two,
):
    anywhere = pl.BlockSpec(memory_space=pl.ANY)
    scalar = pl.BlockSpec(memory_space=pltpu.SMEM)
    dma = pltpu.SemaphoreType.DMA
    vm = pltpu.VMEM
    first, second = pl.pallas_call(
        kernel,
        out_shape=(
            jax.ShapeDtypeStruct((1, B, R), BF),
            jax.ShapeDtypeStruct((C2, B, R), BF),
        ),
        in_specs=[anywhere] * 11 + [scalar] * 2,
        out_specs=(anywhere, anywhere),
        scratch_shapes=[
            vm((B, R), BF),
            vm((NZ, 2, 2, 2, 128, B), BF),
            vm((U // BD, BD, B), BF),
            vm((B, R), BF),
            vm((U // BD, 1, BD), jnp.int32),
            pltpu.SMEM((1, U), jnp.int32),
            vm((C2, U // BD, BD, B), BF),
            vm((C2, B, R), BF),
            vm((UT // BD, C2, BD), jnp.int32),
            pltpu.SMEM((C2, UT), jnp.int32),
            vm((UP // BD, C2, BD), jnp.int32),
            pltpu.SMEM((C2, UP), jnp.int32),
            vm((C2, H, 2 * B), BF),
            vm((S, B), BF),
            pltpu.SMEM((1,), jnp.int32),
            vm((C2, R, B), F32),
            vm((U // BD + LEAVES * B // BS, R, BD), BF),
            vm((C2 + 1, 8, R, B), BF),
            vm((C2, R, B), BF),
            vm((C2, R, B), BF),
            vm((3, 8, R, B), BF),
            vm((B, R), BF),
            vm((C2, B, R), BF),
            dma((27,)), dma((C2 + 1,)),
            dma((7,)), dma((7,)), dma((11,)), dma((11,)), dma((11,)), dma((11,)),
            dma((C2,)), dma((C2,)), dma((C2,)), dma((C2,)), dma((C2 + 1, 2)), dma((C2 + 1, 2)),
            dma((C2,)), dma((C2,)),
            dma((3,)), dma((3,)), dma((3,)), dma((3,)),
            dma((2,)), dma((2,)), dma((3, 3)), dma((3, 3)), dma((3, 4)), dma((3, 4)),
        ],
        compiler_params=pltpu.CompilerParams(
            collective_id=0, has_side_effects=True, vmem_limit_bytes=56 * 1024 * 1024
        ),
        cost_estimate=pl.CostEstimate(flops=20_000_000_000, bytes_accessed=12_000_000, transcendentals=0),
        name="adjoint_solve",
    )(
        top_solution, right_one, update_one.reshape(1, U // BD, BD, B), inverse_one, top_rows_one,
        right_two, update_two.reshape(C2, U // BD, BD, B), inverse_two, top_rows_two, sep_rows,
        live_one, parent, live_two,
    )
    return pl.pallas_call(
        hand_out,
        out_shape=(
            jax.ShapeDtypeStruct((1, B, R), BF),
            jax.ShapeDtypeStruct((C2, B, R), BF),
        ),
        in_specs=[anywhere] * 2,
        out_specs=(anywhere, anywhere),
        scratch_shapes=[pltpu.VMEM((C2 + 1, B, R), BF), dma((PARTS + 1,)), dma((PARTS + 1,))],
        compiler_params=pltpu.CompilerParams(vmem_limit_bytes=56 * 1024 * 1024),
        name="hand_out",
    )(first, second)


def solution(mesh):
    in_specs = (
        P(("leaf", "grid"), None),
        P("leaf", "grid", None),
        P("leaf", None, "grid"),
        P("leaf", None, "grid"),
        P("leaf", None),
        P("leaf"),
        P("leaf", "grid", None),
        P("leaf", None, "grid"),
        P("leaf", None, "grid"),
        P("leaf", None),
        P("leaf", None),
        P("leaf"),
        P("leaf"),
    )
    out_specs = (P("leaf", "grid", None), P("leaf", "grid", None))
    return jax.shard_map(local, mesh=mesh, in_specs=in_specs, out_specs=out_specs, check_vma=False)
```

```python
import functools

import jax
import jax.numpy as jnp
from jax import lax
from jax.experimental import pallas as pl
from jax.experimental.pallas import tpu as pltpu
from jax.sharding import PartitionSpec as P

MESH = pl.DeviceIdType.MESH
F32 = jnp.float32
BF = jnp.bfloat16

R = 256
B = 128
S = 1024
U = 2048
UT = 1536
UP = 512
C2 = 12
NX, NY, NZ = 4, 4, 8
LEAVES = NY * NZ
BS = 256
BD = 256

ONE = C2
H = S // 2
W = 1
LAG_B, LAG_C, LAG_D, LAG_E = 13, 17, 18, 21


def kernel(
    top, right1, upd1, inv1, rows1, right2, upd2, inv2, rows2, seps, live1, parent_s, live2_s,
    out1, out2,
    topb, topT, u1, r1, t1, t1s, u2, r2, t2, t2s, sp, sps, iv, i1, live1_s,
    acc, cum, rbuf, pbuf, pout, s1, ob1, ob2,
    ld, ldsem_out,
    g_send, g_recv, a_send, a_recv, c_send, c_recv,
    i_send, i_recv, x_send, x_recv, k_send, k_recv, p_send, p_recv,
    o_send, o_recv, ok_send, ok_recv,
    nb_send, nb_recv, sx_send, sx_recv, sk_send, sk_recv,
):
    leaf = lax.axis_index("leaf")
    g = lax.axis_index("grid")
    z, y = leaf // NY, leaf % NY
    x, c = g // 2, g % 2
    sib = (leaf, x * 2 + (1 - c))

    def at_x(xx):
        return (leaf, xx * 2 + c)

    def rcopy(src, dst, ssem, rsem, dev):
        return pltpu.make_async_remote_copy(
            src_ref=src, dst_ref=dst, send_sem=ssem, recv_sem=rsem, device_id=dev, device_id_type=MESH
        )

    def same(ref, ssem, rsem, dev):
        return rcopy(ref, ref, ssem, rsem, dev)

    own_rows = topb.at[pl.ds(pl.multiple_of(g * 16, 16), 16), :]
    half = pl.ds(pl.multiple_of(jnp.where(x >= 2, H, 0), H), H)
    loads = [
        (top, own_rows),
        (upd1.at[0], u1),
        (rows1, t1s),
        (right1.at[0], r1),
        (inv1.at[0], i1),
        (live1, live1_s),
        (rows2, t2s),
        (upd2, u2),
        (seps, sps),
        (right2, r2),
        (inv2.at[:, half], iv.at[:, :, pl.ds(0, B)]),
    ]
    loads += [(rows1.at[:, pl.ds(d * BD, BD)], t1.at[d]) for d in range(U // BD)]
    loads += [(rows2.at[:, pl.ds(d * BD, BD)], t2.at[d]) for d in range(UT // BD)]
    loads += [(seps.at[:, pl.ds(d * BD, BD)], sp.at[d]) for d in range(UP // BD)]
    loads = [pltpu.make_async_copy(a, b, ld.at[i]) for i, (a, b) in enumerate(loads)]
    for copy in loads:
        copy.start()

    barrier = pltpu.get_barrier_semaphore()

    def greet(dev):
        pl.semaphore_signal(barrier, inc=1, device_id=dev, device_id_type=MESH)

    for d in range(1, 8):
        greet((leaf, (g + d) % 8))
    for d in range(1, NY):
        greet((z * NY + (y + d) % NY, g))
    for d in range(1, NZ):
        greet((((z + d) % NZ) * NY + y, g))

    @pl.when(leaf > 0)
    def _():
        greet((leaf - 1, g))

    @pl.when(leaf < LEAVES - 1)
    def _():
        greet((leaf + 1, g))

    @pl.when(x == 1)
    def _():
        def zero(f, carry):
            for k in range(2):
                rbuf[f, k] = jnp.zeros((R, B), BF)
            return carry

        lax.fori_loop(0, C2, zero, 0)

    for k in range(6):

        @pl.when(k < 2 * x)
        def _():
            rbuf[ONE, k] = jnp.zeros((R, B), BF)

    ends = jnp.where(leaf > 0, 1, 0) + jnp.where(leaf < LEAVES - 1, 1, 0)
    pl.semaphore_wait(barrier, 7 + (NY - 1) + (NZ - 1) + ends)

    loads[0].wait()
    for d in range(1, 8):
        rcopy(own_rows, own_rows, g_send.at[d - 1], g_recv.at[d - 1], (leaf, (g + d) % 8)).start()
    def ship(f):
        src = inv2.at[f, pl.ds(H, H)]
        return rcopy(src, iv.at[f, :, pl.ds(B, B)], i_send.at[f], i_recv.at[f], at_x(3 - x))

    def each_front(action):
        def one(f, carry):
            action(f)
            return carry

        lax.fori_loop(0, C2, one, 0)

    @pl.when(x < 2)
    def _():
        each_front(lambda f: ship(f).start())

    for d in range(1, 8):
        other = (g + 8 - d) % 8
        part = topb.at[pl.ds(pl.multiple_of(other * 16, 16), 16), :]
        same(part, g_send.at[d - 1], g_recv.at[d - 1], (leaf, other)).wait_recv()
    block = topb[...].astype(F32).T.astype(BF)
    topT[z, y // 2, y % 2] = block.reshape(2, 128, B)

    def yz(zz, yy):
        return (((zz + NZ) % NZ) * NY + (yy + NY) % NY, g)

    def hand(region, i):
        same(region, c_send.at[i], c_recv.at[i], sib).start()

    def block_at(zz, yy, core):
        zz, yy = (zz + NZ) % NZ, (yy + NY) % NY
        return topT.at[zz, yy // 2, yy % 2, core]

    def plane(zz):
        return topT.at[(zz + NZ) % NZ, :, :, 0]

    def half_plane(zz, i):
        return topT.at[(zz + NZ) % NZ, i, :, 0]

    def column(yy):
        yy = (yy + NY) % NY
        return topT.at[:, yy // 2, yy % 2, 1]

    def pieces0():
        out = [block_at(z, y - d, 0) for d in (1, 3, 2)]
        out += [plane(z - 1), plane(z + 1), plane(z - 2), plane(z + 2)]
        return out + [plane(z - 3), plane(z + 3), half_plane(z - 4, 0), half_plane(z + 4, 1)]

    def pieces1():
        return [block_at(z - i, y, 1) for i in range(1, NZ)] + [column(y - d) for d in (1, 3, 2)]

    def send(region, i, dev):
        same(region, a_send.at[i], a_recv.at[i], dev).start()

    def gone(got):
        for i, region in enumerate(got):
            same(region, a_send.at[i], a_recv.at[i], sib).wait_send()
            same(region, c_send.at[i], c_recv.at[i], sib).wait_send()

    def handed(other):
        for i, region in enumerate(other):
            same(region, c_send.at[i], c_recv.at[i], sib).wait_recv()

    def turn_right():
        for copy in loads[1:]:
            copy.wait()

        def one(f, carry):
            acc[f] = r2[f].astype(F32).T
            return carry

        lax.fori_loop(0, C2, one, 0)

    @pl.when(c == 0)
    def _():
        got = pieces0()

        def arrived(i):
            same(got[i], a_send.at[i], a_recv.at[i], sib).wait_recv()

        for i, d in enumerate((1, 3, 2)):
            send(block_at(z, y, 0), i, yz(z, y + d))
        turn_right()
        for i in range(3):
            arrived(i)
        for i, d in ((5, 2), (6, -2), (3, 1), (4, -1)):
            send(plane(z), i, yz(z + d, y))
        for i in range(3):
            hand(got[i], i)
        arrived(5)
        send(plane(z - 2), 7, yz(z + 1, y))
        send(half_plane(z - 2, 0), 9, yz(z + 2, y))
        arrived(6)
        send(plane(z + 2), 8, yz(z - 1, y))
        send(half_plane(z + 2, 1), 10, yz(z - 2, y))
        for i in (3, 4):
            arrived(i)
            hand(got[i], i)
        for i in (5, 6):
            hand(got[i], i)
        for i in (7, 8, 9, 10):
            arrived(i)
            hand(got[i], i)
        handed(pieces1())

    @pl.when(c == 1)
    def _():
        got = pieces1()

        def arrived(i):
            same(got[i], a_send.at[i], a_recv.at[i], sib).wait_recv()

        for i in (4, 3, 5, 2, 6, 1, 7):
            send(block_at(z, y, 1), i - 1, yz(z + i, y))
        turn_right()
        for i in range(7):
            arrived(i)
        for i, d in ((9, 2), (7, 1), (8, 3)):
            send(column(y), i, yz(z, y + d))
        for i in range(7):
            hand(got[i], i)
        for i in (7, 8, 9):
            arrived(i)
            hand(got[i], i)
        handed(pieces0())


    def picked_product(count, pool, front, vec, sca, source, factor):
        nd, ns = count // BD, pool // BS
        total = jnp.zeros((R, B), F32)
        firsts = [sca[front, i * BD] for i in range(1, nd)]
        passed_at = []
        for i, v in enumerate(firsts):
            ends = jnp.int32(i)
            for j in range(1, ns):
                ends = ends + jnp.where(v >= j * BS, 1, 0)
            passed_at.append(ends)
        iota = lax.broadcasted_iota(jnp.int16, (BS, BD), 0)
        steps = nd + ns - 1
        held = None
        for t in range(steps):
            d = jnp.int32(0)
            for ends in passed_at:
                d = d + jnp.where(ends < t, 1, 0)
            s = t - d
            picks = vec[d, pl.ds(front, 1), :]
            onehot = jnp.where(iota == (picks - s * BS).astype(jnp.int16), BF(1), BF(0))
            got = jnp.dot(source(s), onehot, preferred_element_type=F32).astype(BF)
            if t:
                keep = jnp.where(d == held[1], 1.0, 0.0)
                got = got + held[0] * jnp.full((R, BD), keep, F32).astype(BF)
            cum[t] = got
            held = (got, d)
        passed_at.append(steps - 1)
        for d, last in enumerate(passed_at):
            total = total + jnp.dot(cum[last], factor(d), preferred_element_type=F32)
        return total

    def top_rows(s):
        pair = topT[s >> 1, s & 1]
        return jnp.concatenate([pair[i].reshape(R, B) for i in range(2)], axis=1)

    twin = jnp.where(x >= 2, 5 - x, jnp.where(x == 1, 0, 1))
    sends, gets = x >= 1, x != 1

    def xs(f, k, dest):
        return same(rbuf.at[f, 2 * k + c], x_send.at[f], x_recv.at[f], at_x(dest))

    def ks(f, i, k, core):
        return same(rbuf.at[f, 2 * k + core], k_send.at[f, i], k_recv.at[f, i], sib)

    def ps(f):
        return rcopy(pout.at[f], pbuf.at[f], p_send.at[f], p_recv.at[f], at_x(3 - x))

    def own_sends(f):
        @pl.when(sends)
        def _():
            xs(f, x, twin).start()

        ks(f, 0, x, c).start()

    def first_hop(f):
        @pl.when(gets)
        def _():
            xs(f, twin, twin).wait_recv()
            ks(f, 1, twin, c).start()

    def from_core(f):
        ks(f, 0, x, 1 - c).wait_recv()

        @pl.when(gets)
        def _():
            ks(f, 1, twin, 1 - c).wait_recv()

    lanes = lax.broadcasted_iota(jnp.int32, (R, B), 1) + g * B

    def uppers(fronts, outs):
        for f in fronts:
            from_core(f)
            ship(f).wait_recv()
        both = []
        for f in fronts:
            lhs = jnp.concatenate([rbuf[f, 4 + k] for k in range(4)], axis=1)
            both.append(jnp.dot(lhs, iv[f], preferred_element_type=F32))
        for f, value in zip(fronts, both):
            pout[f] = value[:, B:].astype(BF)
        for f in fronts:
            ps(f).start()
        outs(fronts, [value[:, :B] for value in both])

    def lowers(fronts, outs):
        for f in fronts:
            from_core(f)
            ps(f).wait_recv()
        solved = []
        for f in fronts:
            lhs = jnp.concatenate([rbuf[f, k] for k in range(4)], axis=1)
            own = jnp.dot(lhs, iv[f, :, :B], preferred_element_type=F32)
            solved.append(own + pbuf[f].astype(F32))
        outs(fronts, solved)

    total1 = picked_product(U, LEAVES * B, 0, t1, t1s, top_rows, lambda d: u1[d])
    rbuf[ONE, g] = (r1[...].astype(F32).T - total1).astype(BF)

    def o_x(k, dest):
        return same(rbuf.at[ONE, 2 * k + c], o_send.at[dest], o_recv.at[k - 1], at_x(dest))

    def o_k(k, core):
        return same(rbuf.at[ONE, 2 * k + core], ok_send.at[k - 1], ok_recv.at[k - 1], sib)

    def one_sends(act):
        for dest in range(3):
            pl.when(dest < x)(lambda: act(o_x(x, dest)))
        act(ks(ONE, 0, x, c))

    def one_first_hop():
        for k in range(1, 4):

            @pl.when(k > x)
            def _():
                o_x(k, 0).wait_recv()
                o_k(k, c).start()

    def solve_one():
        ks(ONE, 0, x, 1 - c).wait_recv()
        for k in range(1, 4):
            pl.when(k > x)(lambda: o_k(k, 1 - c).wait_recv())
        lhs = jnp.concatenate([rbuf[ONE, k] for k in range(8)], axis=1)
        solved = jnp.dot(lhs, i1[...], preferred_element_type=F32)
        out_one(jnp.where(lanes < live1_s[0], solved, 0.0))

    one_sends(lambda copy: copy.start())

    def s1_x(slot, d):
        return same(s1.at[slot, g], sx_send.at[slot, d - 1], sx_recv.at[slot, d - 1], at_x((x + d) % NX))

    def s1_x_got(slot, d):
        return s1.at[slot, 2 * ((x + NX - d) % NX) + c]

    def s1_k(slot, k, core):
        return same(s1.at[slot, 2 * k + core], sk_send.at[slot, k], sk_recv.at[slot, k], sib)

    def with_slots(slots, body):
        for slot in slots:
            if slot == 1:
                body(slot)
            else:

                @pl.when((leaf > 0) if slot == 0 else (leaf < LEAVES - 1))
                def _():
                    body(slot)

    def s1_up():
        return rcopy(s1.at[1, g], s1.at[0, g], nb_send.at[0], nb_recv.at[0], (leaf + 1, g))

    def s1_down():
        return rcopy(s1.at[1, g], s1.at[2, g], nb_send.at[1], nb_recv.at[1], (leaf - 1, g))

    def out_one(solved):
        s1[1, g] = solved.astype(BF)

        @pl.when(leaf < LEAVES - 1)
        def _():
            s1_up().start()

        @pl.when(leaf > 0)
        def _():
            s1_down().start()

        spread(1)
        ob1[...] = solved.T.astype(BF)
        pltpu.make_async_copy(ob1, out1.at[0], ldsem_out.at[C2]).start()

    def spread(slot):
        def over_x():
            for d in (2, 1, 3):
                s1_x(slot, d).start()

        if slot == 1:
            over_x()
        else:
            pl.when(c == 0)(over_x)
        s1_k(slot, x, c).start()

    def s1_relay(d, act):
        k = 2 * ((x + NX - d) % NX) + c

        @pl.when(leaf < LEAVES - 1)
        def _():
            act(rcopy(s1.at[1, k], s1.at[0, k], sx_send.at[0, d - 1], sx_recv.at[0, d - 1], (leaf + 1, g)))

        @pl.when(leaf > 0)
        def _():
            act(rcopy(s1.at[1, k], s1.at[2, k], sx_send.at[2, d - 1], sx_recv.at[2, d - 1], (leaf - 1, g)))

    def s1_neighbours():
        def body(slot):
            if slot == 0:
                s1_up().wait_recv()
            else:
                s1_down().wait_recv()
            spread(slot)

        with_slots((0, 2), body)

    def s1_cross(slots):
        def body(slot):
            for d in (1, 3, 2):
                same(s1_x_got(slot, d), sx_send.at[slot, d - 1], sx_recv.at[slot, d - 1], sib).wait_recv()
                if slot == 1:
                    pl.when(c == 1)(lambda: s1_relay(d, lambda copy: copy.start()))
                s1_k(slot, (x + NX - d) % NX, c).start()

        with_slots(slots, body)

    def s1_end():
        def body(slot):
            for k in range(NX):
                s1_k(slot, k, 1 - c).wait_recv()

        with_slots((1, 0, 2), body)

    def top_part(f):
        acc[f] = acc[f] - picked_product(UT, LEAVES * B, f, t2, t2s, top_rows, lambda d: u2[f, d])

    def parent_parts(fronts):
        left = []
        for f in fronts:
            slot = jnp.clip(parent_s[f] - leaf + 1, 0, 2)

            def parent_rows(s, slot=slot):
                return jnp.concatenate([s1[slot, 2 * s], s1[slot, 2 * s + 1]], axis=1)

            total = picked_product(UP, S, f, sp, sps, parent_rows, lambda d, f=f: u2[f, UT // BD + d])
            left.append((acc[f] - total).astype(BF))
        for f, value in zip(fronts, left):
            rbuf[f, g] = value
        for f in fronts:
            own_sends(f)

    def out_two(fronts, solved):
        for f, value in zip(fronts, solved):
            ob2[f] = jnp.where(lanes < live2_s[f], value, 0.0).T.astype(BF)
        for f in fronts:
            pltpu.make_async_copy(ob2.at[f], out2.at[f], ldsem_out.at[f]).start()

    def finish(fronts):
        f, = fronts
        ks(f, 0, x, c).wait_send()

        @pl.when(sends)
        def _():
            xs(f, x, twin).wait_send()

        @pl.when(gets)
        def _():
            ks(f, 1, twin, c).wait_send()

        @pl.when(x >= 2)
        def _():
            ps(f).wait_send()


    def early_sends_gone():
        pl.when(c == 0)(lambda: gone(pieces0()))
        pl.when(c == 1)(lambda: gone(pieces1()))

    def later_sends_gone():
        for d in range(1, 8):
            rcopy(own_rows, own_rows, g_send.at[d - 1], g_recv.at[d - 1], (leaf, (g + d) % 8)).wait_send()

        one_sends(lambda copy: copy.wait_send())
        for k in range(1, 4):
            pl.when(k > x)(lambda: o_k(k, c).wait_send())

        @pl.when(x < 2)
        def _():
            each_front(lambda f: ship(f).wait_send())

        def finish_slot(slot):
            def over_x():
                for d in range(1, 4):
                    s1_x(slot, d).wait_send()

            if slot == 1:
                over_x()
            else:
                pl.when(c == 0)(over_x)
            for k in range(NX):
                s1_k(slot, k, c).wait_send()

        @pl.when(c == 1)
        def _():
            for d in range(1, 4):
                s1_relay(d, lambda copy: copy.wait_send())

        with_slots((0, 1, 2), finish_slot)

        @pl.when(leaf < LEAVES - 1)
        def _():
            s1_up().wait_send()

        @pl.when(leaf > 0)
        def _():
            s1_down().wait_send()


    def body(it, carry):
        pl.when(it == 4)(one_first_hop)
        pl.when(it == 5)(solve_one)
        pl.when(it == 8)(s1_neighbours)
        pl.when(it == 9)(lambda: s1_cross((1,)))
        pl.when(it == 12)(lambda: s1_cross((0, 2)))
        pl.when(it == 13)(s1_end)

        def staged(lag, action):
            @pl.when(jnp.logical_and(it >= lag, it < C2 // W + lag))
            def _():
                action([(it - lag) * W + i for i in range(W)])

        def first_hops(fronts):
            for f in fronts:
                first_hop(f)

        def two_upper(fronts):
            pl.when(x >= 2)(lambda: uppers(fronts, out_two))

        def two_lower(fronts):
            pl.when(x < 2)(lambda: lowers(fronts, out_two))

        staged(LAG_C, first_hops)
        staged(LAG_D, two_upper)
        staged(LAG_B, parent_parts)
        staged(LAG_E, two_lower)
        staged(LAG_E + 1, finish)
        pl.when(it == LAG_B + 2)(early_sends_gone)
        pl.when(it == LAG_C + 2)(later_sends_gone)
        pl.when(it < C2)(lambda: top_part(it))
        return carry

    lax.fori_loop(0, C2 + LAG_E + 1, body, 0)

    pltpu.make_async_copy(ob1, out1.at[0], ldsem_out.at[C2]).wait()

    def finish_out(f, carry):
        pltpu.make_async_copy(ob2.at[f], out2.at[f], ldsem_out.at[f]).wait()
        return carry

    lax.fori_loop(0, C2, finish_out, 0)


PARTS = 6


def hand_out(first, second, out1, out2, held, sem_in, sem_out):
    step = C2 // PARTS

    def part(ref, i):
        return ref.at[pl.ds(i * step, step)]

    copies = [
        (
            pltpu.make_async_copy(part(second, i), part(held, i), sem_in.at[i]),
            pltpu.make_async_copy(part(held, i), part(out2, i), sem_out.at[i]),
        )
        for i in range(PARTS)
    ]
    last = held.at[pl.ds(C2, 1)]
    copies.append(
        (
            pltpu.make_async_copy(first, last, sem_in.at[PARTS]),
            pltpu.make_async_copy(last, out1, sem_out.at[PARTS]),
        )
    )
    for get, _ in copies:
        get.start()
    for get, put in copies:
        get.wait()
        put.start()
    for _, put in copies:
        put.wait()


def local(
    top_solution, right_one, update_one, inverse_one, top_rows_one, live_one,
    right_two, update_two, inverse_two, top_rows_two, sep_rows, parent, live_two,
):
    anywhere = pl.BlockSpec(memory_space=pl.ANY)
    scalar = pl.BlockSpec(memory_space=pltpu.SMEM)
    dma = pltpu.SemaphoreType.DMA
    vm = pltpu.VMEM
    first, second = pl.pallas_call(
        kernel,
        out_shape=(
            jax.ShapeDtypeStruct((1, B, R), BF),
            jax.ShapeDtypeStruct((C2, B, R), BF),
        ),
        in_specs=[anywhere] * 11 + [scalar] * 2,
        out_specs=(anywhere, anywhere),
        scratch_shapes=[
            vm((B, R), BF),
            vm((NZ, 2, 2, 2, 128, B), BF),
            vm((U // BD, BD, B), BF),
            vm((B, R), BF),
            vm((U // BD, 1, BD), jnp.int32),
            pltpu.SMEM((1, U), jnp.int32),
            vm((C2, U // BD, BD, B), BF),
            vm((C2, B, R), BF),
            vm((UT // BD, C2, BD), jnp.int32),
            pltpu.SMEM((C2, UT), jnp.int32),
            vm((UP // BD, C2, BD), jnp.int32),
            pltpu.SMEM((C2, UP), jnp.int32),
            vm((C2, H, 2 * B), BF),
            vm((S, B), BF),
            pltpu.SMEM((1,), jnp.int32),
            vm((C2, R, B), F32),
            vm((U // BD + LEAVES * B // BS, R, BD), BF),
            vm((C2 + 1, 8, R, B), BF),
            vm((C2, R, B), BF),
            vm((C2, R, B), BF),
            vm((3, 8, R, B), BF),
            vm((B, R), BF),
            vm((C2, B, R), BF),
            dma((27,)), dma((C2 + 1,)),
            dma((7,)), dma((7,)), dma((11,)), dma((11,)), dma((11,)), dma((11,)),
            dma((C2,)), dma((C2,)), dma((C2,)), dma((C2,)), dma((C2 + 1, 2)), dma((C2 + 1, 2)),
            dma((C2,)), dma((C2,)),
            dma((3,)), dma((3,)), dma((3,)), dma((3,)),
            dma((2,)), dma((2,)), dma((3, 3)), dma((3, 3)), dma((3, 4)), dma((3, 4)),
        ],
        compiler_params=pltpu.CompilerParams(
            collective_id=0, has_side_effects=True, vmem_limit_bytes=56 * 1024 * 1024
        ),
        cost_estimate=pl.CostEstimate(flops=20_000_000_000, bytes_accessed=12_000_000, transcendentals=0),
        name="adjoint_solve",
    )(
        top_solution, right_one, update_one.reshape(1, U // BD, BD, B), inverse_one, top_rows_one,
        right_two, update_two.reshape(C2, U // BD, BD, B), inverse_two, top_rows_two, sep_rows,
        live_one, parent, live_two,
    )
    return pl.pallas_call(
        hand_out,
        out_shape=(
            jax.ShapeDtypeStruct((1, B, R), BF),
            jax.ShapeDtypeStruct((C2, B, R), BF),
        ),
        in_specs=[anywhere] * 2,
        out_specs=(anywhere, anywhere),
        scratch_shapes=[pltpu.VMEM((C2 + 1, B, R), BF), dma((PARTS + 1,)), dma((PARTS + 1,))],
        compiler_params=pltpu.CompilerParams(vmem_limit_bytes=56 * 1024 * 1024),
        name="hand_out",
    )(first, second)


def solution(mesh):
    in_specs = (
        P(("leaf", "grid"), None),
        P("leaf", "grid", None),
        P("leaf", None, "grid"),
        P("leaf", None, "grid"),
        P("leaf", None),
        P("leaf"),
        P("leaf", "grid", None),
        P("leaf", None, "grid"),
        P("leaf", None, "grid"),
        P("leaf", None),
        P("leaf", None),
        P("leaf"),
        P("leaf"),
    )
    out_specs = (P("leaf", "grid", None), P("leaf", "grid", None))
    return jax.shard_map(local, mesh=mesh, in_specs=in_specs, out_specs=out_specs, check_vma=False)
```
